32 devices in a mesh: row: 8 (over y, x, core), col: 4 (over z).
Axes of the slice: x: 2, y: 2, z: 4, core: 2. Of those that a mesh axis runs over, the one named last changes fastest.
Arguments:
- objects: float32 [2, 2, 1024, 1024], P(None, None, 'row', 'col'), as said below
- probe_modes: float32 [4, 2, 128, 128], replicated, may hold values from -3 to 3
- intensities: float32 [8, 4, 2, 128, 128], P('row', 'col'), may hold values from 0 to 2
- positions: int32 [8, 4, 2, 2], P('row', 'col'), may hold values from 0 to 896, as said below
- counts: int32 [8, 4], P('row', 'col'), may hold values from 0 to 2, as said below
Outputs:
- refined_object: float32 [2, 2, 1024, 1024], P(None, None, 'row', 'col')
- refined_probe: float32 [4, 2, 128, 128], replicated
The draws below stay inside these ranges and needn't reach their ends.
Inputs may be any that keep to these rules, and one draw needn't show every extreme that they name: `positions`: for the pattern slot [i, j, k], the row of its top-left pixel plus 128 / 2 lies in [i * 128, (i + 1) * 128) and the column plus 128 / 2 in [j * 256, (j + 1) * 256); every patch lies inside the object; slot 0 of the first tile starts at pixel (0, 0) and slot 0 of the last tile ends at the object's last row and column. The live slots of a tile are its first counts[i, j] slots; some tile has all 2 live and some tile has none. `objects`: every entry lies in [-1.5, 1.5].
All inputs are finite; a program needn't handle non-finite values.
Results may differ from the reference program's by a relative error of at most 0.0003.
Values sent between devices are 32-bit elements; how exact they have to be, the bound alone decides.
A program may use at most 64 MiB of HBM per device.

```python
import math
import jax
import jax.numpy as jnp
from jax import lax

TILE_R = 128
TILE_C = 256
PROBE = 128
MODES = 4
SLICES = 2
ITERS = 2
PAT_DEV = 2
OBJ_R = 1024
OBJ_C = 1024
N_ROW = 8
N_COL = 4


def window_count(marks, reach, axis):
    length = marks.shape[axis]
    pad_shape = [(0, 0), (0, 0)]
    pad_shape[axis] = (reach, reach)
    padded = jnp.pad(marks, pad_shape)
    running = jnp.cumsum(padded, axis=axis, dtype=jnp.int32)
    zero_shape = list(marks.shape)
    zero_shape[axis] = 1
    running = jnp.concatenate([jnp.zeros(zero_shape, jnp.int32), running], axis=axis)
    upper = lax_slice(running, 2 * reach + 1, length, axis)
    lower = lax_slice(running, 0, length, axis)
    return upper - lower


def lax_slice(array, start, length, axis):
    if axis == 0:
        return array[start:start + length, :]
    return array[:, start:start + length]


def draw_objects(key, part):
    base = jax.random.uniform(key, (SLICES, 2, OBJ_R, OBJ_C), jnp.float32)
    lower = jnp.array([0.6, -0.4], jnp.float32)
    spread = jnp.array([0.8, 0.8], jnp.float32)
    dark = 0.5
    corners = draw_positions(key, part).reshape(-1, 2)
    margin = PROBE // 2
    reach = max(PROBE // 8, 1)
    center_rows = corners[:, 0] + margin
    center_cols = corners[:, 1] + margin
    marks = jnp.zeros((OBJ_R, OBJ_C), jnp.int32).at[center_rows, center_cols].add(1)
    boxed = window_count(window_count(marks, reach, 0), reach, 1)
    factor = jnp.where(boxed > 0, dark, 1.0).astype(jnp.float32)
    field = lower[None, :, None, None] + spread[None, :, None, None] * base
    return field * factor[None, None, :, :]


def draw_counts(key, part):
    row_tiles = OBJ_R // TILE_R
    col_tiles = OBJ_C // TILE_C
    tiles = row_tiles * col_tiles
    first_key = jax.random.fold_in(key, 11)
    second_key = jax.random.fold_in(key, 12)
    values = jax.random.randint(first_key, (tiles,), 0, PAT_DEV + 1)
    chosen = jax.random.randint(second_key, (), 0, tiles)
    empty_tile = (chosen + 1) % tiles
    tile_ids = jnp.arange(tiles)
    values = jnp.where(tile_ids == chosen, PAT_DEV, values)
    values = jnp.where(tile_ids == empty_tile, 0, values)
    return values.reshape(row_tiles, col_tiles).astype(jnp.int32)


def draw_positions(key, part):
    row_tiles = OBJ_R // TILE_R
    col_tiles = OBJ_C // TILE_C
    margin = PROBE // 2
    row_start = jnp.arange(row_tiles, dtype=jnp.int32) * TILE_R
    col_start = jnp.arange(col_tiles, dtype=jnp.int32) * TILE_C
    row_lower = jnp.maximum(row_start, margin)
    row_upper = jnp.minimum(row_start + TILE_R, OBJ_R - margin + 1)
    col_lower = jnp.maximum(col_start, margin)
    col_upper = jnp.minimum(col_start + TILE_C, OBJ_C - margin + 1)
    shape = (row_tiles, col_tiles, PAT_DEV)
    row_centers = jax.random.randint(jax.random.fold_in(key, 21), shape, row_lower[:, None, None], row_upper[:, None, None])
    col_centers = jax.random.randint(jax.random.fold_in(key, 22), shape, col_lower[None, :, None], col_upper[None, :, None])
    row_ids = jnp.arange(row_tiles, dtype=jnp.int32)[:, None, None]
    col_ids = jnp.arange(col_tiles, dtype=jnp.int32)[None, :, None]
    slot_ids = jnp.arange(PAT_DEV, dtype=jnp.int32)[None, None, :]
    first_slot = (row_ids == 0) & (col_ids == 0) & (slot_ids == 0)
    last_slot = (row_ids == row_tiles - 1) & (col_ids == col_tiles - 1) & (slot_ids == 0)
    row_centers = jnp.where(first_slot, margin, row_centers)
    col_centers = jnp.where(first_slot, margin, col_centers)
    row_centers = jnp.where(last_slot, OBJ_R - margin, row_centers)
    col_centers = jnp.where(last_slot, OBJ_C - margin, col_centers)
    return jnp.stack([row_centers - margin, col_centers - margin], axis=-1).astype(jnp.int32)


def level_of(own_key, shape, cuts, smallest, top_value):
    loudness, own = 1.0, jax.random.fold_in(own_key, 6)
    for position, blocks in cuts:
        draws = jnp.exp(jax.random.uniform(jax.random.fold_in(own, position), (blocks,), jnp.float32, smallest / len(cuts), top_value / len(cuts)))
        loudness = loudness * jnp.repeat(draws, shape[position] // blocks).reshape([-1 if axis == position else 1 for axis in range(len(shape))])
    return loudness


def centred(stream_key, extent, scale, limit, held_as=jnp.bfloat16):
    result = scale * jax.random.normal(stream_key, extent, jnp.float32)
    return jnp.clip(result, min=-limit, max=limit).astype(held_as)


def setup_inputs(seed: int = 0) -> dict:
    streams_of = jax.random.split(jax.random.key(seed), 6)
    objects = draw_objects(jax.random.fold_in(streams_of[5], 71), 0)
    probe_modes = centred(streams_of[1], (MODES, 2, PROBE, PROBE), 0.5, 3.0, jnp.float32)
    intensities = jnp.clip(2.0 * jax.random.uniform(streams_of[2], (N_ROW, N_COL, PAT_DEV, PROBE, PROBE), jnp.float32) ** level_of(streams_of[2], (N_ROW, N_COL, PAT_DEV, PROBE, PROBE), ((0, 8), (1, 4)), -0.2, 0.2), 0.0, 2.0)
    positions = draw_positions(jax.random.fold_in(streams_of[5], 71), 0)
    counts = draw_counts(jax.random.fold_in(streams_of[5], 71), 0)
    return dict(objects=objects, probe_modes=probe_modes, intensities=intensities, positions=positions, counts=counts)


highest = lax.Precision.HIGHEST

def block_table(upper_left, upper_right, lower_left, lower_right):
    return jnp.stack([jnp.stack([upper_left, upper_right]), jnp.stack([lower_left, lower_right])])

def fourier_tables(width):
    index = jnp.arange(width, dtype=jnp.int32)
    product = index[:, None] * index[None, :] % width
    angle = product.astype(jnp.float32) * (-2.0 * math.pi / width)
    scale = 1.0 / math.sqrt(width)
    middle = width // 2
    frequency = ((index + middle) % width - middle).astype(jnp.float32)
    phase = (frequency[:, None] ** 2 + frequency[None, :] ** 2) * (-4.0 * math.pi / (width * width))
    cosine = jnp.cos(angle) * scale
    sine = jnp.sin(angle) * scale
    forward_left = block_table(cosine, -sine, sine, cosine)
    forward_right = block_table(cosine, sine, -sine, cosine)
    inverse_left = block_table(cosine, sine, -sine, cosine)
    inverse_right = block_table(cosine, -sine, sine, cosine)
    return (forward_left, forward_right, inverse_left, inverse_right, jnp.cos(phase), jnp.sin(phase))

def fourier_field(field, tables, direction):
    if direction > 0:
        left_table, right_table = (tables[0], tables[1])
    else:
        left_table, right_table = (tables[2], tables[3])
    upper = jnp.einsum('pqab,kmqbc->kmpac', left_table, field, precision=highest)
    return jnp.einsum('kmqab,qpbc->kmpac', upper, right_table, precision=highest)

def complex_product(first, second):
    real_part = first[:, :, 0] * second[:, :, 0] - first[:, :, 1] * second[:, :, 1]
    imag_part = first[:, :, 0] * second[:, :, 1] + first[:, :, 1] * second[:, :, 0]
    return jnp.stack([real_part, imag_part], axis=2)

def conj_product(first, second):
    real_part = first[:, :, 0] * second[:, :, 0] + first[:, :, 1] * second[:, :, 1]
    imag_part = first[:, :, 0] * second[:, :, 1] - first[:, :, 1] * second[:, :, 0]
    return jnp.stack([real_part, imag_part], axis=2)

def propagate(field, tables, direction):
    spectrum = fourier_field(field, tables, 1.0)
    kernel = jnp.stack([tables[4], tables[5] * direction])[None, None]
    return fourier_field(complex_product(spectrum, kernel), tables, -1.0)

def pattern_terms(probe_modes, patches, measured, live_mask, tables):
    slot_count = patches.shape[0]
    layers = patches.shape[1]
    wave = jnp.broadcast_to(probe_modes[None], (slot_count,) + probe_modes.shape)
    inputs = []
    for layer_index in range(layers):
        obj = patches[:, layer_index][:, None]
        inputs.append(wave)
        exit_wave = complex_product(wave, obj)
        if layer_index < layers - 1:
            wave = propagate(exit_wave, tables, 1.0)
        else:
            far = fourier_field(exit_wave, tables, 1.0)
    intensity = lax.optimization_barrier(jnp.sum(far * far, axis=(1, 2)))
    weight = (2.0 * (intensity - measured))[:, None, None]
    grad = fourier_field(weight * far, tables, -1.0)
    slice_grads = [None] * layers
    for layer_index in reversed(range(layers)):
        obj = patches[:, layer_index][:, None]
        slice_grads[layer_index] = lax.optimization_barrier(jnp.sum(conj_product(inputs[layer_index], grad), axis=1))
        back = conj_product(obj, grad)
        if layer_index > 0:
            grad = propagate(back, tables, -1.0)
    weights = live_mask[:, None, None, None, None]
    object_grads = jnp.stack(slice_grads, axis=1) * weights
    probe_terms = lax.optimization_barrier(jnp.sum(back * weights, axis=0))
    first = patches[:, 0]
    illumination = lax.optimization_barrier(jnp.sum(lax.optimization_barrier(jnp.sum(first * first, axis=1)) * live_mask[:, None, None], axis=0))
    return (object_grads, probe_terms, illumination)

def reference(objects, probe_modes, intensities, positions, counts):
    width = probe_modes.shape[-1]
    layers = objects.shape[0]
    tables = fourier_tables(width)
    slot_count = intensities.shape[2]
    tiles = counts.shape[0] * counts.shape[1]
    tile_corners = positions.reshape(tiles, slot_count, 2).astype(jnp.int32)
    tile_measured = intensities.reshape(tiles, slot_count, width, width)
    slot_ids = jnp.arange(slot_count, dtype=jnp.int32)
    tile_live = (slot_ids[None, :] < counts.reshape(tiles, 1)).astype(jnp.float32)
    for step_index in range(ITERS):
        current = objects
        modes_now = probe_modes

        def tile_step(carry, inputs):
            grad_field, probe_sum, light_sum = carry
            corners, measured, live_mask = inputs

            def cut_patch(corner):
                start = (jnp.int32(0), jnp.int32(0), corner[0].astype(jnp.int32), corner[1].astype(jnp.int32))
                return lax.dynamic_slice(current, start, (layers, 2, width, width))
            patches = jax.vmap(cut_patch)(corners)
            object_grads, probe_terms, illumination = pattern_terms(modes_now, patches, measured, live_mask, tables)

            def place(slot_index, field):
                corner = corners[slot_index]
                start = (jnp.int32(0), jnp.int32(0), corner[0].astype(jnp.int32), corner[1].astype(jnp.int32))
                present = lax.dynamic_slice(field, start, (layers, 2, width, width))
                return lax.dynamic_update_slice(field, present + object_grads[slot_index], start)
            grad_field = lax.fori_loop(0, slot_count, place, grad_field)
            return ((grad_field, probe_sum + probe_terms, light_sum + illumination), None)
        start_carry = (jnp.zeros(current.shape, jnp.float32), jnp.zeros(modes_now.shape, jnp.float32), jnp.zeros((width, width), jnp.float32))
        (grad_field, probe_sum, light_sum), _ = lax.scan(tile_step, start_carry, (tile_corners, tile_measured, tile_live))
        objects = current - 0.1 * grad_field
        probe_modes = modes_now - 0.25 * probe_sum / jnp.sqrt(light_sum)
    return (objects, probe_modes)
```

```python
import functools
import math

import jax
import jax.numpy as jnp
import ml_dtypes
import numpy as np
from jax import lax
from jax.experimental import pallas as pl
from jax.experimental.pallas import tpu as pltpu
from jax.sharding import PartitionSpec as P

ITERS = 2
VMEM_BYTES = 48 * 1024 * 1024
MESH = pl.DeviceIdType.MESH
DIRS = ((-1, 0), (1, 0), (0, -1), (0, 1), (-1, -1), (-1, 1), (1, -1), (1, 1))


def real_block(table):
    return np.block([[table.real, -table.imag], [table.imag, table.real]])


def transform_tables(width):
    index = np.arange(width)
    product = np.outer(index, index) % width
    far = np.exp(-2j * math.pi * product / width) / math.sqrt(width)
    frequency = (index + width // 2) % width - width // 2
    factor = np.exp(-4j * math.pi * frequency.astype(np.float64) ** 2 / width**2)
    step = far.conj() @ (factor[:, None] * far)
    step = (step + step.T) / 2
    blocks = np.stack([real_block(far), real_block(far).T, real_block(step), real_block(step).T])
    high = blocks.astype(ml_dtypes.bfloat16)
    low = (blocks - high.astype(np.float64)).astype(ml_dtypes.bfloat16)
    return np.stack([high, low], axis=1)


def split_parts(value):
    high = value.astype(jnp.bfloat16)
    return high, (value - high.astype(jnp.float32)).astype(jnp.bfloat16)


def dot(first, second):
    return jnp.dot(first, second, preferred_element_type=jnp.float32)


def apply_transform(tab_ref, left, fields):
    right = left + 1 if left % 2 == 0 else left - 1
    width = fields[0][0].shape[0]
    stacked = jnp.concatenate([jnp.concatenate([r, i], axis=0) for r, i in fields], axis=1)
    high, low = split_parts(stacked)
    t_high, t_low = tab_ref[left, 0], tab_ref[left, 1]
    upper = dot(t_high, high) + dot(t_high, low) + dot(t_low, high)
    rows = []
    for m in range(len(fields)):
        cols = slice(m * width, (m + 1) * width)
        rows.append(jnp.concatenate([upper[:width, cols], upper[width:, cols]], axis=1))
    high, low = split_parts(jnp.concatenate(rows, axis=0))
    t_high, t_low = tab_ref[right, 0], tab_ref[right, 1]
    out = dot(high, t_high) + dot(low, t_high) + dot(high, t_low)
    return [
        (out[m * width : (m + 1) * width, :width], out[m * width : (m + 1) * width, width:])
        for m in range(len(fields))
    ]


def times(a, b):
    return (a[0] * b[0] - a[1] * b[1], a[0] * b[1] + a[1] * b[0])


def conj_times(a, b):
    return (a[0] * b[0] + a[1] * b[1], a[0] * b[1] - a[1] * b[0])


def pass_kernel(
    tile, pos_ref, cnt_ref, center_ref, left_ref, right_ref, modes_ref, meas_ref, tab_ref,
    grad_ref, gl_ref, gr_ref, sums_ref, ext,
):
    tile_rows, tile_cols = tile
    width = meas_ref.shape[-1]
    half = width // 2
    slots = meas_ref.shape[0]
    modes = modes_ref.shape[0] // 2
    last = width + tile_cols
    ext[:, :, width:last] = center_ref[...]
    for q in range(2):
        ext[q, :, :width] = pltpu.roll(left_ref[q], half, 1)
        ext[q + 2, :, :width] = left_ref[q]
        ext[q, :, last:] = right_ref[q]
        ext[q + 2, :, last:] = pltpu.roll(right_ref[q], half, 1)
    grad_ref[...] = jnp.zeros_like(grad_ref)
    sums_ref[...] = jnp.zeros_like(sums_ref)
    row0 = lax.axis_index("row") * tile_rows - half
    col0 = lax.axis_index("col") * tile_cols - width
    lane = lax.broadcasted_iota(jnp.int32, (width, width), 1)
    tall_lane = lax.broadcasted_iota(jnp.int32, (width + 8, width), 1)

    def slot(k, carry):
        @pl.when(k < cnt_ref[0, 0])
        def _():
            row = pos_ref[k, 0] - row0
            col = pos_ref[k, 1] - col0
            base = pl.multiple_of((col // width) * width, width)
            shift = col % width
            top = pl.multiple_of((row // 8) * 8, 8)
            down = row % 8
            up = (width + 8 - down) % (width + 8)
            back_shift = (width - shift) % width

            def cut(p):
                window = ext[p, pl.ds(top, width + 8), pl.ds(base, 2 * width)]
                window = pltpu.roll(window, up, 0)[:width]
                first = pltpu.roll(window[:, :width], back_shift, 1)
                second = pltpu.roll(window[:, width:], back_shift, 1)
                return jnp.where(lane < width - shift, first, second)

            o0 = (cut(0), cut(1))
            o1 = (cut(2), cut(3))
            probe = [(modes_ref[2 * m], modes_ref[2 * m + 1]) for m in range(modes)]
            waves = apply_transform(tab_ref, 2, [times(p, o0) for p in probe])
            far = apply_transform(tab_ref, 0, [times(w, o1) for w in waves])
            intensity = sum(r * r + i * i for r, i in far)
            weight = 2.0 * (intensity - meas_ref[k])
            grads = apply_transform(tab_ref, 1, [(weight * r, weight * i) for r, i in far])

            def add_patch(p, value):
                value = jnp.concatenate([value, jnp.zeros((8, width), jnp.float32)], axis=0)
                rolled = pltpu.roll(pltpu.roll(value, down, 0), shift, 1)
                rows = pl.ds(top, width + 8)
                grad_ref[p, rows, pl.ds(base, width)] += jnp.where(tall_lane >= shift, rolled, 0.0)
                after = pl.multiple_of(base + width, width)
                grad_ref[p, rows, pl.ds(after, width)] += jnp.where(tall_lane < shift, rolled, 0.0)

            terms = [conj_times(w, g) for w, g in zip(waves, grads)]
            add_patch(2, sum(t[0] for t in terms))
            add_patch(3, sum(t[1] for t in terms))
            grads = apply_transform(tab_ref, 3, [conj_times(o1, g) for g in grads])
            terms = [conj_times(p, g) for p, g in zip(probe, grads)]
            add_patch(0, sum(t[0] for t in terms))
            add_patch(1, sum(t[1] for t in terms))
            for m in range(modes):
                back = conj_times(o0, grads[m])
                sums_ref[2 * m] += back[0]
                sums_ref[2 * m + 1] += back[1]
            sums_ref[2 * modes] += o0[0] * o0[0] + o0[1] * o0[1]

        return carry

    lax.fori_loop(0, slots, slot, 0)
    lane = lax.broadcasted_iota(jnp.int32, (grad_ref.shape[1], width), 1)
    for q in range(2):
        gl_ref[q] = jnp.where(
            lane < half, pltpu.roll(grad_ref[q, :, :width], half, 1), grad_ref[q + 2, :, :width]
        )
        gr_ref[q] = jnp.where(
            lane < half, grad_ref[q, :, last:], pltpu.roll(grad_ref[q + 2, :, last:], half, 1)
        )


def local_pass(extended, modes, measured, positions, counts, tables, tile):
    center, left, right = extended
    rows = center.shape[1]
    width = measured.shape[-1]
    wide = center.shape[2] + 2 * width
    smem = pl.BlockSpec(memory_space=pltpu.SMEM)
    vmem = pl.BlockSpec(memory_space=pltpu.VMEM)
    shape = lambda *s: jax.ShapeDtypeStruct(s, jnp.float32)
    return pl.pallas_call(
        functools.partial(pass_kernel, tile),
        out_shape=(
            shape(4, rows, wide),
            shape(2, rows, width),
            shape(2, rows, width),
            shape(modes.shape[0] + 1, width, width),
        ),
        in_specs=[smem, smem] + [vmem] * 6,
        out_specs=(vmem,) * 4,
        scratch_shapes=[pltpu.VMEM((4, rows, wide), jnp.float32)],
        compiler_params=pltpu.CompilerParams(vmem_limit_bytes=VMEM_BYTES),
        name="local_pass",
    )(positions, counts, center, left, right, modes, measured, tables)


class Neighbours:
    def __init__(self, sizes, me, pieces, send_sems, recv_sems):
        self.sizes, self.me, self.pieces = sizes, me, pieces
        self.send_sems, self.recv_sems = send_sems, recv_sems

    def there(self, dr, dc):
        (rows, cols), (r, c) = self.sizes, self.me
        found = None
        for cond in (
            [r > 0] if dr < 0 else [r < rows - 1] if dr > 0 else []
        ) + ([c > 0] if dc < 0 else [c < cols - 1] if dc > 0 else []):
            found = cond if found is None else jnp.logical_and(found, cond)
        return found

    def copy(self, d):
        dr, dc = DIRS[d]
        src, dst = self.pieces[d]
        return pltpu.make_async_remote_copy(
            src_ref=src, dst_ref=dst, send_sem=self.send_sems.at[d], recv_sem=self.recv_sems.at[d],
            device_id=(self.me[0] + dr, self.me[1] + dc), device_id_type=MESH,
        )

    def start(self):
        for d, (dr, dc) in enumerate(DIRS):
            @pl.when(self.there(dr, dc))
            def _(d=d):
                self.copy(d).start()

    def wait_recv(self, after=None):
        for d, (dr, dc) in enumerate(DIRS):
            @pl.when(self.there(-dr, -dc))
            def _(d=d):
                self.copy(d).wait_recv()
                if after is not None:
                    after(d)

    def wait_send(self):
        for d, (dr, dc) in enumerate(DIRS):
            @pl.when(self.there(dr, dc))
            def _(d=d):
                self.copy(d).wait_send()


def reduce_stages(sizes, width):
    stages, size = [], width
    for axis in range(2):
        mask = 1
        while mask < sizes[axis]:
            halves = axis == 0 and size >= 16
            size = size // 2 if halves else size
            stages.append((axis, mask, size, halves))
            mask *= 2
    return stages


def exchange_kernel(sizes, has_sums, has_halo, stages, row_off, *refs):
    refs = list(refs)
    take = lambda n: [refs.pop(0) for _ in range(n)]
    (obj_ref,) = take(1)
    if has_sums:
        grad_ref, gl_ref, gr_ref, sums_ref, modes_ref = take(5)
    if has_halo:
        center_ref, left_ref, right_ref = take(3)
    else:
        (out_ref,) = take(1)
    if has_sums:
        (new_modes_ref,) = take(1)
    if has_halo:
        pack_l, pack_r, halo_send, halo_recv = take(4)
    if has_sums:
        total, from_u, from_d, from_l, from_r, from_ul, from_ur, from_dl, from_dr = take(9)
        rim_send, rim_recv, acc, ar_send, ar_recv, ag_send, ag_recv = take(7)
        landing = refs

    r, c = lax.axis_index("row"), lax.axis_index("col")
    me = (r, c)
    if has_halo:
        tile_rows, tile_cols = center_ref.shape[1] // 2, center_ref.shape[2]
        width = left_ref.shape[-1]
    else:
        tile_rows, tile_cols = out_ref.shape[1], out_ref.shape[2]
        width = gl_ref.shape[-1]
    half = width // 2
    lane = lax.broadcasted_iota(jnp.int32, (tile_rows, width), 1)

    def partner(axis, mask):
        bit = (me[axis] // mask) % 2
        other = me[axis] + mask * (1 - 2 * bit)
        return bit, ((other, c) if axis == 0 else (r, other))

    near = Neighbours(sizes, me, None, None, None)
    barrier = pltpu.get_barrier_semaphore()
    expected = 0
    for dr, dc in DIRS:
        cond = near.there(dr, dc)
        expected = expected + cond.astype(jnp.int32)

        @pl.when(cond)
        def _(dr=dr, dc=dc):
            pl.semaphore_signal(barrier, inc=1, device_id=(r + dr, c + dc), device_id_type=MESH)

    if has_sums:
        for axis, mask, _, _ in stages:
            _, device = partner(axis, mask)
            pl.semaphore_signal(barrier, inc=1, device_id=device, device_id_type=MESH)
            expected = expected + 1
    pl.semaphore_wait(barrier, expected)

    if has_sums:
        top, bottom = slice(0, half), slice(tile_rows + half, tile_rows + width)
        inner = slice(half, tile_rows + half)
        cols = slice(width, width + tile_cols)
        rims = Neighbours(sizes, me, [
            (grad_ref.at[:, top, cols], from_d),
            (grad_ref.at[:, bottom, cols], from_u),
            (gl_ref.at[:, inner, :], from_r),
            (gr_ref.at[:, inner, :], from_l),
            (gl_ref.at[:, top, :], from_dr),
            (gr_ref.at[:, top, :], from_dl),
            (gl_ref.at[:, bottom, :], from_ur),
            (gr_ref.at[:, bottom, :], from_ul),
        ], rim_send, rim_recv)
        rims.start()

        offs = [jnp.int32(0)]
        for axis, mask, size, halves in stages:
            bit, _ = partner(axis, mask)
            offs.append(offs[-1] + bit * size if halves else offs[-1])

        def rows_at(off, size):
            return pl.ds(pl.multiple_of(off, 8), size)

        def reduce_copy(s):
            axis, mask, size, halves = stages[s]
            bit, device = partner(axis, mask)
            sent = offs[s] + (1 - bit) * size if halves else offs[s]
            source = sums_ref if s == 0 else acc
            return pltpu.make_async_remote_copy(
                src_ref=source.at[:, rows_at(sent, size), :], dst_ref=landing[s],
                send_sem=ar_send.at[s], recv_sem=ar_recv.at[s], device_id=device, device_id_type=MESH,
            )

        def reduce_finish(s):
            reduce_copy(s).wait()
            kept = rows_at(offs[s + 1], stages[s][2])
            source = sums_ref if s == 0 else acc
            acc[:, kept, :] = source[:, kept, :] + landing[s][...]

        reduce_copy(0).start()
        reduce_finish(0)
        reduce_copy(1).start()
        total[...] = grad_ref[:, inner, cols]

        def add_rim(d):
            if d == 0:
                total[:, tile_rows - half :, :] += from_d[...]
            elif d == 1:
                total[:, :half, :] += from_u[...]
            else:
                source, rows = {
                    2: (from_r, slice(0, tile_rows)), 3: (from_l, slice(0, tile_rows)),
                    4: (from_dr, slice(tile_rows - half, tile_rows)),
                    5: (from_dl, slice(tile_rows - half, tile_rows)),
                    6: (from_ur, slice(0, half)), 7: (from_ul, slice(0, half)),
                }[d]
                side = lane[rows]
                for q in range(2):
                    value = source[q]
                    turned = pltpu.roll(value, half, 1)
                    if d in (3, 5, 7):
                        total[q, rows, :width] += jnp.where(side < half, value, 0.0)
                        total[q + 2, rows, :width] += jnp.where(side < half, turned, 0.0)
                    else:
                        total[q, rows, tile_cols - width :] += jnp.where(side >= half, turned, 0.0)
                        total[q + 2, rows, tile_cols - width :] += jnp.where(side >= half, value, 0.0)

        rims.wait_recv(add_rim)
        new = obj_ref[:, row_off : row_off + tile_rows, :] - 0.1 * total[...]
    else:
        new = obj_ref[...]

    if has_halo:
        center_ref[:, half : half + tile_rows, :] = new
        for q in range(2):
            lower, upper = new[q], new[q + 2]
            pack_l[q] = jnp.where(lane < half, lower[:, :width], pltpu.roll(upper[:, :width], half, 1))
            pack_r[q] = jnp.where(
                lane < half, pltpu.roll(lower[:, tile_cols - width :], half, 1), upper[:, tile_cols - width :]
            )
        first, final = slice(0, half), slice(tile_rows + half, tile_rows + width)
        middle = slice(half, half + tile_rows)
        ends = slice(tile_rows - half, tile_rows)
        halos = Neighbours(sizes, me, [
            (center_ref.at[:, half:width, :], center_ref.at[:, final, :]),
            (center_ref.at[:, tile_rows : tile_rows + half, :], center_ref.at[:, first, :]),
            (pack_l, right_ref.at[:, middle, :]),
            (pack_r, left_ref.at[:, middle, :]),
            (pack_l.at[:, first, :], right_ref.at[:, final, :]),
            (pack_r.at[:, first, :], left_ref.at[:, final, :]),
            (pack_l.at[:, ends, :], right_ref.at[:, first, :]),
            (pack_r.at[:, ends, :], left_ref.at[:, first, :]),
        ], halo_send, halo_recv)
        halos.start()
    else:
        out_ref[...] = new

    if has_sums:
        reduce_finish(1)
        for s in range(2, len(stages)):
            reduce_copy(s).start()
            reduce_finish(s)
        planes = modes_ref.shape[0]
        kept = rows_at(offs[-1], stages[-1][2])
        scale = 0.25 / jnp.sqrt(acc[planes, kept, :])
        new_modes_ref[:, kept, :] = modes_ref[:, kept, :] - acc[:planes, kept, :] * scale[None]
        for s in reversed(range(len(stages))):
            axis, mask, size, halves = stages[s]
            if halves:
                _, device = partner(axis, mask)
                part = new_modes_ref.at[:, rows_at(offs[s + 1], size), :]
                copy = pltpu.make_async_remote_copy(
                    src_ref=part, dst_ref=part, send_sem=ag_send.at[s], recv_sem=ag_recv.at[s],
                    device_id=device, device_id_type=MESH,
                )
                copy.start()
                copy.wait()
        rims.wait_send()
    if has_halo:
        halos.wait_recv()
        halos.wait_send()


def exchange(sizes, tile, width, ident, obj, sums=None, halo=True, row_off=0):
    tile_rows, tile_cols = tile
    half = width // 2
    rows = tile_rows + width
    vmem = pl.BlockSpec(memory_space=pltpu.VMEM)
    shape = lambda *s: jax.ShapeDtypeStruct(s, jnp.float32)
    buf = lambda *s: pltpu.VMEM(s, jnp.float32)
    dma = lambda n: pltpu.SemaphoreType.DMA((n,))
    operands, outs, scratch, stages = [obj], [], [], []
    if halo:
        outs += [shape(4, rows, tile_cols), shape(2, rows, width), shape(2, rows, width)]
        scratch += [buf(2, tile_rows, width), buf(2, tile_rows, width), dma(8), dma(8)]
    else:
        outs += [shape(4, tile_rows, tile_cols)]
    if sums is not None:
        operands += list(sums)
        planes = sums[-1].shape[0]
        outs += [shape(planes, width, width)]
        stages = reduce_stages(sizes, width)
        scratch += [
            buf(4, tile_rows, tile_cols),
            buf(4, half, tile_cols), buf(4, half, tile_cols),
            buf(2, tile_rows, width), buf(2, tile_rows, width),
            buf(2, half, width), buf(2, half, width), buf(2, half, width), buf(2, half, width),
            dma(8), dma(8),
            buf(planes + 1, width, width),
            dma(len(stages)), dma(len(stages)), dma(len(stages)), dma(len(stages)),
        ] + [buf(planes + 1, size, width) for _, _, size, _ in stages]
    return pl.pallas_call(
        functools.partial(exchange_kernel, sizes, sums is not None, halo, stages, row_off),
        out_shape=tuple(outs),
        in_specs=[vmem] * len(operands),
        out_specs=(vmem,) * len(outs),
        scratch_shapes=scratch,
        compiler_params=pltpu.CompilerParams(
            collective_id=ident, has_side_effects=True, vmem_limit_bytes=VMEM_BYTES
        ),
        name="exchange_%d" % ident,
    )(*operands)


def body(sizes, objects, probe_modes, intensities, positions, counts):
    width = probe_modes.shape[-1]
    tile = objects.shape[2:]
    modes = probe_modes.reshape(-1, width, width)
    tables = jnp.asarray(transform_tables(width))
    objects4 = objects.reshape((4,) + tile)
    extended = exchange(sizes, tile, width, 0, objects4)
    for step in range(ITERS):
        final = step == ITERS - 1
        sums = local_pass(extended, modes, intensities[0, 0], positions[0, 0], counts, tables, tile)
        result = exchange(
            sizes, tile, width, step + 1, extended[0], tuple(sums) + (modes,),
            halo=not final, row_off=width // 2,
        )
        modes = result[-1]
        extended = result[:-1]
    return extended[0].reshape(objects.shape), modes.reshape(probe_modes.shape)


def solution(mesh):
    sizes = (mesh.shape["row"], mesh.shape["col"])
    return jax.shard_map(
        functools.partial(body, sizes),
        mesh=mesh,
        in_specs=(
            P(None, None, "row", "col"),
            P(),
            P("row", "col", None, None, None),
            P("row", "col", None, None),
            P("row", "col"),
        ),
        out_specs=(P(None, None, "row", "col"), P()),
        check_vma=False,
    )
```

```python
import functools
import math

import jax
import jax.numpy as jnp
import ml_dtypes
import numpy as np
from jax import lax
from jax.experimental import pallas as pl
from jax.experimental.pallas import tpu as pltpu
from jax.sharding import PartitionSpec as P

ITERS = 2
PASS_BYTES = 32 * 1024 * 1024
EXCHANGE_BYTES = 24 * 1024 * 1024
MESH = pl.DeviceIdType.MESH
DIRS = ((-1, 0), (1, 0), (0, -1), (0, 1), (-1, -1), (-1, 1), (1, -1), (1, 1))


def real_block(table):
    return np.block([[table.real, -table.imag], [table.imag, table.real]])


def transform_tables(width):
    index = np.arange(width)
    product = np.outer(index, index) % width
    far = np.exp(-2j * math.pi * product / width) / math.sqrt(width)
    frequency = (index + width // 2) % width - width // 2
    factor = np.exp(-4j * math.pi * frequency.astype(np.float64) ** 2 / width**2)
    step = far.conj() @ (factor[:, None] * far)
    step = (step + step.T) / 2
    blocks = np.stack([real_block(far), real_block(far).T, real_block(step), real_block(step).T])
    parts = []
    for _ in range(3):
        parts.append(blocks.astype(ml_dtypes.bfloat16))
        blocks = blocks - parts[-1].astype(np.float64)
    return np.stack(parts, axis=1)


def split_parts(value):
    high = value.astype(jnp.bfloat16)
    return high, (value - high.astype(jnp.float32)).astype(jnp.bfloat16)


def dot(first, second):
    return jnp.dot(first, second, preferred_element_type=jnp.float32)


def products(tab_ref, place, value, table_first, exact):
    high, low = split_parts(value)
    pairs = [(0, high), (0, low), (1, high)] + ([(2, high)] if exact else [])
    total = None
    for part, operand in pairs:
        table = tab_ref[place, part]
        term = dot(table, operand) if table_first else dot(operand, table)
        total = term if total is None else total + term
    return total


def apply_transform(tab_ref, left, fields, exact):
    right = left + 1 if left % 2 == 0 else left - 1
    width = fields[0][0].shape[0]
    stacked = jnp.concatenate([jnp.concatenate([r, i], axis=0) for r, i in fields], axis=1)
    upper = products(tab_ref, left, stacked, True, exact)
    rows = []
    for m in range(len(fields)):
        cols = slice(m * width, (m + 1) * width)
        rows.append(jnp.concatenate([upper[:width, cols], upper[width:, cols]], axis=1))
    out = products(tab_ref, right, jnp.concatenate(rows, axis=0), False, exact)
    return [
        (out[m * width : (m + 1) * width, :width], out[m * width : (m + 1) * width, width:])
        for m in range(len(fields))
    ]


def times(a, b):
    return (a[0] * b[0] - a[1] * b[1], a[0] * b[1] + a[1] * b[0])


def conj_times(a, b):
    return (a[0] * b[0] + a[1] * b[1], a[0] * b[1] - a[1] * b[0])


def pass_kernel(
    tile, exact, pos_ref, cnt_ref, center_ref, left_ref, right_ref, modes_ref, meas_ref, tab_ref,
    grad_ref, gl_ref, gr_ref, sums_ref, ext,
):
    tile_rows, tile_cols = tile
    width = meas_ref.shape[-1]
    half = width // 2
    slots = meas_ref.shape[0]
    modes = modes_ref.shape[0] // 2
    last = width + tile_cols
    ext[:, :, width:last] = center_ref[...]
    for q in range(2):
        ext[q, :, :width] = pltpu.roll(left_ref[q], half, 1)
        ext[q + 2, :, :width] = left_ref[q]
        ext[q, :, last:] = right_ref[q]
        ext[q + 2, :, last:] = pltpu.roll(right_ref[q], half, 1)
    grad_ref[...] = jnp.zeros_like(grad_ref)
    sums_ref[...] = jnp.zeros_like(sums_ref)
    row0 = lax.axis_index("row") * tile_rows - half
    col0 = lax.axis_index("col") * tile_cols - width
    lane = lax.broadcasted_iota(jnp.int32, (width, width), 1)
    tall_lane = lax.broadcasted_iota(jnp.int32, (width + 8, width), 1)

    def slot(k, carry):
        @pl.when(k < cnt_ref[0, 0])
        def _():
            row = pos_ref[k, 0] - row0
            col = pos_ref[k, 1] - col0
            base = pl.multiple_of((col // width) * width, width)
            shift = col % width
            top = pl.multiple_of((row // 8) * 8, 8)
            down = row % 8
            up = (width + 8 - down) % (width + 8)
            back_shift = (width - shift) % width

            def cut(p):
                window = ext[p, pl.ds(top, width + 8), pl.ds(base, 2 * width)]
                window = pltpu.roll(window, up, 0)[:width]
                first = pltpu.roll(window[:, :width], back_shift, 1)
                second = pltpu.roll(window[:, width:], back_shift, 1)
                return jnp.where(lane < width - shift, first, second)

            o0 = (cut(0), cut(1))
            o1 = (cut(2), cut(3))
            probe = [(modes_ref[2 * m], modes_ref[2 * m + 1]) for m in range(modes)]
            waves = apply_transform(tab_ref, 2, [times(p, o0) for p in probe], exact)
            far = apply_transform(tab_ref, 0, [times(w, o1) for w in waves], exact)
            intensity = sum(r * r + i * i for r, i in far)
            weight = 2.0 * (intensity - meas_ref[k])
            grads = apply_transform(tab_ref, 1, [(weight * r, weight * i) for r, i in far], exact)

            def add_patch(p, value):
                value = jnp.concatenate([value, jnp.zeros((8, width), jnp.float32)], axis=0)
                rolled = pltpu.roll(pltpu.roll(value, down, 0), shift, 1)
                rows = pl.ds(top, width + 8)
                grad_ref[p, rows, pl.ds(base, width)] += jnp.where(tall_lane >= shift, rolled, 0.0)
                after = pl.multiple_of(base + width, width)
                grad_ref[p, rows, pl.ds(after, width)] += jnp.where(tall_lane < shift, rolled, 0.0)

            terms = [conj_times(w, g) for w, g in zip(waves, grads)]
            add_patch(2, sum(t[0] for t in terms))
            add_patch(3, sum(t[1] for t in terms))
            grads = apply_transform(tab_ref, 3, [conj_times(o1, g) for g in grads], exact)
            terms = [conj_times(p, g) for p, g in zip(probe, grads)]
            add_patch(0, sum(t[0] for t in terms))
            add_patch(1, sum(t[1] for t in terms))
            for m in range(modes):
                back = conj_times(o0, grads[m])
                sums_ref[2 * m] += back[0]
                sums_ref[2 * m + 1] += back[1]
            sums_ref[2 * modes] += o0[0] * o0[0] + o0[1] * o0[1]

        return carry

    lax.fori_loop(0, slots, slot, 0)
    lane = lax.broadcasted_iota(jnp.int32, (grad_ref.shape[1], width), 1)
    for q in range(2):
        gl_ref[q] = jnp.where(
            lane < half, pltpu.roll(grad_ref[q, :, :width], half, 1), grad_ref[q + 2, :, :width]
        )
        gr_ref[q] = jnp.where(
            lane < half, grad_ref[q, :, last:], pltpu.roll(grad_ref[q + 2, :, last:], half, 1)
        )


def local_pass(extended, modes, measured, positions, counts, tables, tile, exact):
    center, left, right = extended
    rows = center.shape[1]
    width = measured.shape[-1]
    wide = center.shape[2] + 2 * width
    smem = pl.BlockSpec(memory_space=pltpu.SMEM)
    vmem = pl.BlockSpec(memory_space=pltpu.VMEM)
    shape = lambda *s: jax.ShapeDtypeStruct(s, jnp.float32)
    return pl.pallas_call(
        functools.partial(pass_kernel, tile, exact),
        out_shape=(
            shape(4, rows, wide),
            shape(2, rows, width),
            shape(2, rows, width),
            shape(modes.shape[0] + 1, width, width),
        ),
        in_specs=[smem, smem] + [vmem] * 6,
        out_specs=(vmem,) * 4,
        scratch_shapes=[pltpu.VMEM((4, rows, wide), jnp.float32)],
        compiler_params=pltpu.CompilerParams(vmem_limit_bytes=PASS_BYTES),
        name="local_pass",
    )(positions, counts, center, left, right, modes, measured, tables)


class Neighbours:
    def __init__(self, sizes, me, pieces, send_sems, recv_sems):
        self.sizes, self.me, self.pieces = sizes, me, pieces
        self.send_sems, self.recv_sems = send_sems, recv_sems

    def there(self, dr, dc):
        (rows, cols), (r, c) = self.sizes, self.me
        found = None
        for cond in (
            [r > 0] if dr < 0 else [r < rows - 1] if dr > 0 else []
        ) + ([c > 0] if dc < 0 else [c < cols - 1] if dc > 0 else []):
            found = cond if found is None else jnp.logical_and(found, cond)
        return found

    def copy(self, d):
        dr, dc = DIRS[d]
        src, dst = self.pieces[d]
        return pltpu.make_async_remote_copy(
            src_ref=src, dst_ref=dst, send_sem=self.send_sems.at[d], recv_sem=self.recv_sems.at[d],
            device_id=(self.me[0] + dr, self.me[1] + dc), device_id_type=MESH,
        )

    def start(self):
        for d, (dr, dc) in enumerate(DIRS):
            @pl.when(self.there(dr, dc))
            def _(d=d):
                self.copy(d).start()

    def wait_recv(self, after=None):
        for d, (dr, dc) in enumerate(DIRS):
            @pl.when(self.there(-dr, -dc))
            def _(d=d):
                self.copy(d).wait_recv()
                if after is not None:
                    after(d)

    def wait_send(self):
        for d, (dr, dc) in enumerate(DIRS):
            @pl.when(self.there(dr, dc))
            def _(d=d):
                self.copy(d).wait_send()


def reduce_stages(sizes, width, planes, col_early):
    groups = [[], []]
    for axis in range(2):
        mask, left = 1, sizes[axis]
        while left > 1:
            radix = 4 if left % 4 == 0 and not (axis == 0 and mask == 1) else 2
            groups[axis].append((axis, mask, radix))
            mask, left = mask * radix, left // radix
    first = 1 if col_early else len(groups[0])
    stages, rows = [], width
    for axis, mask, radix in groups[0][:first] + groups[1] + groups[0][first:]:
        kind = "full"
        if axis == 0 and rows % (8 * radix) == 0:
            kind, rows = "rows", rows // radix
        elif axis == 1 and planes % radix == 0:
            kind, planes = "planes", planes // radix
        stages.append((axis, mask, radix, kind, rows, planes))
    return stages


def held_shape(stages, s, width, light):
    _, _, _, _, rows, planes = stages[s]
    if s + 1 < len(stages) and stages[s + 1][3] == "planes":
        radix = stages[s + 1][2]
        return (radix, planes // radix + light, rows, width)
    return (planes + light, rows, width)


class ProbeSum:
    def __init__(self, me, stages, sums_ref, light, scale_ref, modes_ref, new_ref, landing, held, sems):
        self.me, self.stages, self.light, self.scale_ref = me, stages, light, scale_ref
        self.modes_ref, self.new_ref = modes_ref, new_ref
        self.landing, self.held = landing, [sums_ref] + list(held)
        self.send_sem, self.recv_sem, self.spread_send, self.spread_recv = sems
        self.digits, self.where, self.pending = [], [(jnp.int32(0), jnp.int32(0))], []
        for axis, mask, radix, kind, rows, planes in stages:
            digit = (me[axis] // mask) % radix
            row_off, plane_off = self.where[-1]
            if kind == "rows":
                row_off = row_off + digit * rows
            elif kind == "planes":
                plane_off = plane_off + digit * planes
            self.digits.append(digit)
            self.where.append((row_off, plane_off))

    def partner(self, s, j):
        axis, mask, radix = self.stages[s][:3]
        other = (self.digits[s] + j) % radix
        place = self.me[axis] + mask * (other - self.digits[s])
        return other, ((place, self.me[1]) if axis == 0 else (self.me[0], place))

    def piece(self, s, digit):
        kind, rows = self.stages[s][3:5]
        source = self.held[s]
        if kind == "rows":
            return source.at[:, pl.ds(pl.multiple_of(digit * rows, 8), rows), :]
        return source.at[digit] if kind == "planes" else source

    def copy(self, s, j):
        kind = self.stages[s][3]
        other, device = self.partner(s, j)
        slot = self.digits[s] if kind == "full" else j - 1
        return pltpu.make_async_remote_copy(
            src_ref=self.piece(s, other), dst_ref=self.landing[s].at[slot],
            send_sem=self.send_sem.at[s, j - 1], recv_sem=self.recv_sem.at[s, j - 1],
            device_id=device, device_id_type=MESH,
        )

    def start(self, s):
        for j in range(1, self.stages[s][2]):
            copy = self.copy(s, j)
            copy.start()
            self.pending.append(copy)

    def finish(self, s):
        _, _, radix, kind, _, planes = self.stages[s]
        own = self.piece(s, self.digits[s])[...]
        landing = self.landing[s]
        if kind == "full":
            landing[self.digits[s]] = own
        for j in range(1, radix):
            self.copy(s, j).wait_recv()
        if kind == "full":
            value = sum(landing[i] for i in range(radix))
        else:
            value = own + sum(landing[i] for i in range(radix - 1))
        target = self.held[s + 1]
        if s + 1 < len(self.stages) and self.stages[s + 1][3] == "planes":
            groups = self.stages[s + 1][2]
            each = planes // groups
            for g in range(groups):
                target[g, :each] = value[g * each : (g + 1) * each]
                if self.light:
                    target[g, each] = value[planes]
        else:
            target[...] = value

    def region(self, s):
        row_off, plane_off = self.where[s + 1]
        rows, planes = self.stages[s][4:]
        return pl.ds(plane_off, planes), pl.ds(pl.multiple_of(row_off, 8), rows), slice(None)

    def update(self):
        final = len(self.stages) - 1
        value = self.held[-1]
        planes = self.stages[final][5]
        place = self.region(final)
        if self.light:
            self.scale_ref[...] = 0.25 / jnp.sqrt(value[planes])
        self.new_ref[place] = self.modes_ref[place] - value[:planes] * self.scale_ref[...][None]

    def spread_stages(self):
        return [s for s in reversed(range(len(self.stages))) if self.stages[s][3] != "full"]

    def spread_copies(self, s):
        part = self.new_ref.at[self.region(s)]
        return [
            pltpu.make_async_remote_copy(
                src_ref=part, dst_ref=part, send_sem=self.spread_send.at[s, j - 1],
                recv_sem=self.spread_recv.at[s, j - 1], device_id=self.partner(s, j)[1], device_id_type=MESH,
            )
            for j in range(1, self.stages[s][2])
        ]

    def spread_start(self, s):
        copies = self.spread_copies(s)
        for copy in copies:
            copy.start()
        self.pending += copies

    def spread_finish(self, s):
        for copy in self.spread_copies(s):
            copy.wait_recv()

    def drain(self):
        for copy in self.pending:
            copy.wait_send()


def exchange_kernel(sizes, has_sums, has_halo, stages, row_off, *refs):
    refs = list(refs)
    take = lambda n: [refs.pop(0) for _ in range(n)]
    (obj_ref,) = take(1)
    if has_sums:
        grad_ref, gl_ref, gr_ref, sums_ref, modes_ref = take(5)
    if has_halo:
        center_ref, left_ref, right_ref = take(3)
    else:
        (out_ref,) = take(1)
    if has_sums:
        (new_modes_ref,) = take(1)
    if has_halo:
        pack_l, pack_r, halo_send, halo_recv = take(4)
    if has_sums:
        total, from_u, from_d, from_l, from_r, from_ul, from_ur, from_dl, from_dr = take(9)
        rim_send, rim_recv = take(2)
        (scale_ref,) = take(1)
        scratch = [(take(4), take(len(part)), take(len(part))) for part in stages]

    r, c = lax.axis_index("row"), lax.axis_index("col")
    me = (r, c)
    if has_halo:
        tile_rows, tile_cols = center_ref.shape[1] // 2, center_ref.shape[2]
        width = left_ref.shape[-1]
    else:
        tile_rows, tile_cols = out_ref.shape[1], out_ref.shape[2]
        width = gl_ref.shape[-1]
    half = width // 2
    lane = lax.broadcasted_iota(jnp.int32, (tile_rows, width), 1)

    near = Neighbours(sizes, me, None, None, None)
    barrier = pltpu.get_barrier_semaphore()
    expected = 0
    for dr, dc in DIRS:
        cond = near.there(dr, dc)
        expected = expected + cond.astype(jnp.int32)

        @pl.when(cond)
        def _(dr=dr, dc=dc):
            pl.semaphore_signal(barrier, inc=1, device_id=(r + dr, c + dc), device_id_type=MESH)

    if has_sums:
        planes = modes_ref.shape[0]
        cut = planes // 2
        parts = []
        for part, first, last in ((0, cut, planes), (1, 0, cut)):
            sems, landing, held = scratch[part]
            light = 1 - part
            parts.append(ProbeSum(
                me, stages[part], sums_ref.at[first : last + light], light, scale_ref,
                modes_ref.at[first:last], new_modes_ref.at[first:last], landing, held, sems,
            ))
        for s in range(len(stages[0])):
            for j in range(1, stages[0][s][2]):
                _, device = parts[0].partner(s, j)
                pl.semaphore_signal(barrier, inc=1, device_id=device, device_id_type=MESH)
                expected = expected + 1
    pl.semaphore_wait(barrier, expected)

    if has_sums:
        top, bottom = slice(0, half), slice(tile_rows + half, tile_rows + width)
        inner = slice(half, tile_rows + half)
        cols = slice(width, width + tile_cols)
        rims = Neighbours(sizes, me, [
            (grad_ref.at[:, top, cols], from_d),
            (grad_ref.at[:, bottom, cols], from_u),
            (gl_ref.at[:, inner, :], from_r),
            (gr_ref.at[:, inner, :], from_l),
            (gl_ref.at[:, top, :], from_dr),
            (gr_ref.at[:, top, :], from_dl),
            (gl_ref.at[:, bottom, :], from_ur),
            (gr_ref.at[:, bottom, :], from_ul),
        ], rim_send, rim_recv)
        count = len(stages[0])
        if has_halo:
            rims.start()
        for part in parts:
            part.start(0)
        for part in parts:
            part.finish(0)
            if count > 1:
                part.start(1)
        if not has_halo:
            rims.start()
        total[...] = grad_ref[:, inner, cols]

        def add_rim(d):
            if d == 0:
                total[:, tile_rows - half :, :] += from_d[...]
            elif d == 1:
                total[:, :half, :] += from_u[...]
            else:
                source, rows = {
                    2: (from_r, slice(0, tile_rows)), 3: (from_l, slice(0, tile_rows)),
                    4: (from_dr, slice(tile_rows - half, tile_rows)),
                    5: (from_dl, slice(tile_rows - half, tile_rows)),
                    6: (from_ur, slice(0, half)), 7: (from_ul, slice(0, half)),
                }[d]
                side = lane[rows]
                for q in range(2):
                    value = source[q]
                    turned = pltpu.roll(value, half, 1)
                    if d in (3, 5, 7):
                        total[q, rows, :width] += jnp.where(side < half, value, 0.0)
                        total[q + 2, rows, :width] += jnp.where(side < half, turned, 0.0)
                    else:
                        total[q, rows, tile_cols - width :] += jnp.where(side >= half, turned, 0.0)
                        total[q + 2, rows, tile_cols - width :] += jnp.where(side >= half, value, 0.0)

        def reduce_step(s):
            for part in parts:
                part.finish(s)
                if s + 1 < count:
                    part.start(s + 1)

        def spread_step(n):
            for part, order in zip(parts, orders):
                if n == 0:
                    part.update()
                else:
                    part.spread_finish(order[n - 1])
                if n < len(order):
                    part.spread_start(order[n])

        orders = [part.spread_stages() for part in parts]
        early = 2 if has_halo else count
        for s in range(1, early):
            reduce_step(s)
        if not has_halo:
            spread_step(0)
        rims.wait_recv(add_rim)
        new = obj_ref[:, row_off : row_off + tile_rows, :] - 0.1 * total[...]
    else:
        new = obj_ref[...]

    if has_halo:
        center_ref[:, half : half + tile_rows, :] = new
        for q in range(2):
            lower, upper = new[q], new[q + 2]
            pack_l[q] = jnp.where(lane < half, lower[:, :width], pltpu.roll(upper[:, :width], half, 1))
            pack_r[q] = jnp.where(
                lane < half, pltpu.roll(lower[:, tile_cols - width :], half, 1), upper[:, tile_cols - width :]
            )
        first, final = slice(0, half), slice(tile_rows + half, tile_rows + width)
        middle = slice(half, half + tile_rows)
        ends = slice(tile_rows - half, tile_rows)
        halos = Neighbours(sizes, me, [
            (center_ref.at[:, half:width, :], center_ref.at[:, final, :]),
            (center_ref.at[:, tile_rows : tile_rows + half, :], center_ref.at[:, first, :]),
            (pack_l, right_ref.at[:, middle, :]),
            (pack_r, left_ref.at[:, middle, :]),
            (pack_l.at[:, first, :], right_ref.at[:, final, :]),
            (pack_r.at[:, first, :], left_ref.at[:, final, :]),
            (pack_l.at[:, ends, :], right_ref.at[:, first, :]),
            (pack_r.at[:, ends, :], left_ref.at[:, first, :]),
        ], halo_send, halo_recv)
        halos.start()
    else:
        out_ref[...] = new

    if has_sums:
        for s in range(early, count):
            reduce_step(s)
        for n in range(0 if has_halo else 1, len(orders[0]) + 1):
            spread_step(n)
        for part in parts:
            part.drain()
        rims.wait_send()
    if has_halo:
        halos.wait_recv()
        halos.wait_send()


def exchange(sizes, tile, width, ident, obj, sums=None, halo=True, row_off=0):
    tile_rows, tile_cols = tile
    half = width // 2
    rows = tile_rows + width
    vmem = pl.BlockSpec(memory_space=pltpu.VMEM)
    shape = lambda *s: jax.ShapeDtypeStruct(s, jnp.float32)
    buf = lambda *s: pltpu.VMEM(s, jnp.float32)
    dma = lambda *n: pltpu.SemaphoreType.DMA(n)
    operands, outs, scratch, stages = [obj], [], [], []
    specs = [vmem]
    if halo:
        outs += [shape(4, rows, tile_cols), shape(2, rows, width), shape(2, rows, width)]
    else:
        outs += [shape(4, tile_rows, tile_cols)]
    if halo:
        scratch += [buf(2, tile_rows, width), buf(2, tile_rows, width), dma(8), dma(8)]
    if sums is not None:
        operands += list(sums)
        specs += [vmem] * len(sums)
        planes = sums[-1].shape[0]
        outs += [shape(planes, width, width)]
        stages = [reduce_stages(sizes, width, planes // 2, col_early) for col_early in (False, True)]
        scratch += [
            buf(4, tile_rows, tile_cols),
            buf(4, half, tile_cols), buf(4, half, tile_cols),
            buf(2, tile_rows, width), buf(2, tile_rows, width),
            buf(2, half, width), buf(2, half, width), buf(2, half, width), buf(2, half, width),
            dma(8), dma(8), buf(stages[0][-1][4], width),
        ]
        for part, light in zip(stages, (1, 0)):
            scratch += [dma(len(part), 3) for _ in range(4)]
            for _, _, radix, kind, rows_held, planes_held in part:
                slots = radix if kind == "full" else radix - 1
                scratch.append(buf(slots, planes_held + light, rows_held, width))
            scratch += [buf(*held_shape(part, s, width, light)) for s in range(len(part))]
    return pl.pallas_call(
        functools.partial(exchange_kernel, sizes, sums is not None, halo, stages, row_off),
        out_shape=tuple(outs),
        in_specs=specs,
        out_specs=(vmem,) * len(outs),
        scratch_shapes=scratch,
        compiler_params=pltpu.CompilerParams(
            collective_id=ident, has_side_effects=True, vmem_limit_bytes=EXCHANGE_BYTES
        ),
        cost_estimate=pl.CostEstimate(flops=0, transcendentals=0, bytes_accessed=32 * 1024 * 1024),
        name="exchange_%d" % ident,
    )(*operands)


def body(sizes, objects, probe_modes, intensities, positions, counts):
    width = probe_modes.shape[-1]
    tile = objects.shape[2:]
    tables = jnp.asarray(transform_tables(width))
    modes = probe_modes.reshape(-1, width, width)
    measured = intensities[0, 0]
    extended = exchange(sizes, tile, width, 0, objects.reshape((4,) + tile))
    for step in range(ITERS):
        final = step == ITERS - 1
        sums = local_pass(
            extended, modes, measured, positions[0, 0], counts, tables, tile, exact=not final
        )
        result = exchange(
            sizes, tile, width, step + 1, extended[0], tuple(sums) + (modes,),
            halo=not final, row_off=width // 2,
        )
        modes = result[-1]
        extended = result[:-1]
    return extended[0].reshape(objects.shape), modes.reshape(probe_modes.shape)


def solution(mesh):
    sizes = (mesh.shape["row"], mesh.shape["col"])
    return jax.shard_map(
        functools.partial(body, sizes),
        mesh=mesh,
        in_specs=(
            P(None, None, "row", "col"),
            P(),
            P("row", "col", None, None, None),
            P("row", "col", None, None),
            P("row", "col"),
        ),
        out_specs=(P(None, None, "row", "col"), P()),
        check_vma=False,
    )
```

```python
import functools
import math

import jax
import jax.numpy as jnp
import ml_dtypes
import numpy as np
from jax import lax
from jax.experimental import pallas as pl
from jax.experimental.pallas import tpu as pltpu
from jax.sharding import PartitionSpec as P

ITERS = 2
EIGHT = 8.0
PASS_BYTES = 32 * 1024 * 1024
EXCHANGE_BYTES = 24 * 1024 * 1024
MESH = pl.DeviceIdType.MESH
DIRS = ((-1, 0), (1, 0), (0, -1), (0, 1), (-1, -1), (-1, 1), (1, -1), (1, 1))


def real_block(table):
    return np.block([[table.real, -table.imag], [table.imag, table.real]])


def transform_tables(width):
    index = np.arange(width)
    product = np.outer(index, index) % width
    turns = np.exp(-2j * math.pi * product / width)
    far = turns / math.sqrt(width)
    frequency = (index + width // 2) % width - width // 2
    factor = np.exp(-4j * math.pi * frequency.astype(np.float64) ** 2 / width**2)
    step = far.conj() @ (factor[:, None] * far)
    step = (step + step.T) / 2
    blocks = np.stack([real_block(turns / EIGHT), real_block(turns / EIGHT).T, real_block(step), real_block(step).T])
    parts = []
    for _ in range(3):
        parts.append(blocks.astype(ml_dtypes.bfloat16))
        blocks = blocks - parts[-1].astype(np.float64)
    return np.stack(parts, axis=1)


def split_parts(value):
    high = value.astype(jnp.bfloat16)
    return high, (value - high.astype(jnp.float32)).astype(jnp.bfloat16)


def dot(first, second):
    return jnp.dot(first, second, preferred_element_type=jnp.float32)


def products(tab_ref, place, value, table_first, exact):
    high, low = split_parts(value)
    pairs = [(0, high), (0, low), (1, high)] + ([(2, high)] if exact else [])
    total = None
    for part, operand in pairs:
        table = tab_ref[place, part]
        term = dot(table, operand) if table_first else dot(operand, table)
        total = term if total is None else total + term
    return total


def apply_transform(tab_ref, left, fields, exact):
    right = left + 1 if left % 2 == 0 else left - 1
    width = fields[0][0].shape[0]
    stacked = jnp.concatenate([jnp.concatenate([r, i], axis=0) for r, i in fields], axis=1)
    upper = products(tab_ref, left, stacked, True, exact)
    rows = []
    for m in range(len(fields)):
        cols = slice(m * width, (m + 1) * width)
        rows.append(jnp.concatenate([upper[:width, cols], upper[width:, cols]], axis=1))
    out = products(tab_ref, right, jnp.concatenate(rows, axis=0), False, exact)
    return [
        (out[m * width : (m + 1) * width, :width], out[m * width : (m + 1) * width, width:])
        for m in range(len(fields))
    ]


def times(a, b):
    return (a[0] * b[0] - a[1] * b[1], a[0] * b[1] + a[1] * b[0])


def conj_times(a, b):
    return (a[0] * b[0] + a[1] * b[1], a[0] * b[1] - a[1] * b[0])


def pass_kernel(
    tile, exact, pos_ref, cnt_ref, center_ref, left_ref, right_ref, modes_ref, meas_ref, tab_ref,
    grad_ref, gl_ref, gr_ref, sums_ref, ext,
):
    tile_rows, tile_cols = tile
    width = meas_ref.shape[-1]
    half = width // 2
    slots = meas_ref.shape[0]
    modes = modes_ref.shape[0] // 2
    last = width + tile_cols
    ext[:, :, width:last] = center_ref[...]
    for q in range(2):
        ext[q, :, :width] = pltpu.roll(left_ref[q], half, 1)
        ext[q + 2, :, :width] = left_ref[q]
        ext[q, :, last:] = right_ref[q]
        ext[q + 2, :, last:] = pltpu.roll(right_ref[q], half, 1)
    grad_ref[...] = jnp.zeros_like(grad_ref)
    sums_ref[...] = jnp.zeros_like(sums_ref)
    row0 = lax.axis_index("row") * tile_rows - half
    col0 = lax.axis_index("col") * tile_cols - width
    lane = lax.broadcasted_iota(jnp.int32, (width, width), 1)
    tall_lane = lax.broadcasted_iota(jnp.int32, (width + 8, width), 1)

    factor = EIGHT * EIGHT / width
    probe = lambda: [(modes_ref[2 * m], modes_ref[2 * m + 1]) for m in range(modes)]

    class Slot:
        def __init__(self, k):
            self.k = k
            row = pos_ref[k, 0] - row0
            col = pos_ref[k, 1] - col0
            self.base = pl.multiple_of((col // width) * width, width)
            self.shift = col % width
            self.top = pl.multiple_of((row // 8) * 8, 8)
            self.down = row % 8
            self.o0 = (self.cut(0), self.cut(1))
            self.o1 = (self.cut(2), self.cut(3))

        def cut(self, p):
            window = ext[p, pl.ds(self.top, width + 8), pl.ds(self.base, 2 * width)]
            window = pltpu.roll(window, (width + 8 - self.down) % (width + 8), 0)[:width]
            back = (width - self.shift) % width
            first = pltpu.roll(window[:, :width], back, 1)
            second = pltpu.roll(window[:, width:], back, 1)
            return jnp.where(lane < width - self.shift, first, second)

        def add_patch(self, p, value):
            value = jnp.concatenate([value, jnp.zeros((8, width), jnp.float32)], axis=0)
            rolled = pltpu.roll(pltpu.roll(value, self.down, 0), self.shift, 1)
            rows = pl.ds(self.top, width + 8)
            grad_ref[p, rows, pl.ds(self.base, width)] += jnp.where(tall_lane >= self.shift, rolled, 0.0)
            after = pl.multiple_of(self.base + width, width)
            grad_ref[p, rows, pl.ds(after, width)] += jnp.where(tall_lane < self.shift, rolled, 0.0)

        def forward(self):
            self.waves = apply_transform(tab_ref, 2, [times(p, self.o0) for p in probe()], exact)

        def far_field(self):
            self.far = apply_transform(tab_ref, 0, [times(w, self.o1) for w in self.waves], False)

        def far_back(self):
            intensity = sum(r * r + i * i for r, i in self.far) * (factor * factor)
            weight = (2.0 * factor * factor) * (intensity - meas_ref[self.k])
            fields = [(weight * r, weight * i) for r, i in self.far]
            self.grads = apply_transform(tab_ref, 1, fields, False)

        def back(self):
            terms = [conj_times(w, g) for w, g in zip(self.waves, self.grads)]
            self.add_patch(2, sum(t[0] for t in terms))
            self.add_patch(3, sum(t[1] for t in terms))
            fields = [conj_times(self.o1, g) for g in self.grads]
            self.grads = apply_transform(tab_ref, 3, fields, False)

        def finish(self):
            terms = [conj_times(p, g) for p, g in zip(probe(), self.grads)]
            self.add_patch(0, sum(t[0] for t in terms))
            self.add_patch(1, sum(t[1] for t in terms))
            for m in range(modes):
                term = conj_times(self.o0, self.grads[m])
                sums_ref[2 * m] += term[0]
                sums_ref[2 * m + 1] += term[1]
            sums_ref[2 * modes] += self.o0[0] * self.o0[0] + self.o0[1] * self.o0[1]

    def run(indices):
        group = [Slot(k) for k in indices]
        for phase in (Slot.forward, Slot.far_field, Slot.far_back, Slot.back, Slot.finish):
            for one in group:
                phase(one)

    count = cnt_ref[0, 0]

    @pl.when(count == slots)
    def _():
        run(range(slots))

    @pl.when(count < slots)
    def _():
        def alone(k, carry):
            @pl.when(k < count)
            def _():
                run([k])

            return carry

        lax.fori_loop(0, slots - 1, alone, 0)

    lane = lax.broadcasted_iota(jnp.int32, (grad_ref.shape[1], width), 1)
    for q in range(2):
        gl_ref[q] = jnp.where(
            lane < half, pltpu.roll(grad_ref[q, :, :width], half, 1), grad_ref[q + 2, :, :width]
        )
        gr_ref[q] = jnp.where(
            lane < half, grad_ref[q, :, last:], pltpu.roll(grad_ref[q + 2, :, last:], half, 1)
        )


def local_pass(extended, modes, measured, positions, counts, tables, tile, exact):
    center, left, right = extended
    rows = center.shape[1]
    width = measured.shape[-1]
    wide = center.shape[2] + 2 * width
    smem = pl.BlockSpec(memory_space=pltpu.SMEM)
    vmem = pl.BlockSpec(memory_space=pltpu.VMEM)
    shape = lambda *s: jax.ShapeDtypeStruct(s, jnp.float32)
    return pl.pallas_call(
        functools.partial(pass_kernel, tile, exact),
        out_shape=(
            shape(4, rows, wide),
            shape(2, rows, width),
            shape(2, rows, width),
            shape(modes.shape[0] + 1, width, width),
        ),
        in_specs=[smem, smem] + [vmem] * 6,
        out_specs=(vmem,) * 4,
        scratch_shapes=[pltpu.VMEM((4, rows, wide), jnp.float32)],
        compiler_params=pltpu.CompilerParams(vmem_limit_bytes=PASS_BYTES),
        name="local_pass",
    )(positions, counts, center, left, right, modes, measured, tables)


class Neighbours:
    def __init__(self, sizes, me, pieces, send_sems, recv_sems):
        self.sizes, self.me, self.pieces = sizes, me, pieces
        self.send_sems, self.recv_sems = send_sems, recv_sems

    def there(self, dr, dc):
        (rows, cols), (r, c) = self.sizes, self.me
        found = None
        for cond in (
            [r > 0] if dr < 0 else [r < rows - 1] if dr > 0 else []
        ) + ([c > 0] if dc < 0 else [c < cols - 1] if dc > 0 else []):
            found = cond if found is None else jnp.logical_and(found, cond)
        return found

    def copy(self, d):
        dr, dc = DIRS[d]
        src, dst = self.pieces[d]
        return pltpu.make_async_remote_copy(
            src_ref=src, dst_ref=dst, send_sem=self.send_sems.at[d], recv_sem=self.recv_sems.at[d],
            device_id=(self.me[0] + dr, self.me[1] + dc), device_id_type=MESH,
        )

    def start(self):
        for d, (dr, dc) in enumerate(DIRS):
            @pl.when(self.there(dr, dc))
            def _(d=d):
                self.copy(d).start()

    def wait_recv(self, after=None):
        for d, (dr, dc) in enumerate(DIRS):
            @pl.when(self.there(-dr, -dc))
            def _(d=d):
                self.copy(d).wait_recv()
                if after is not None:
                    after(d)

    def wait_send(self):
        for d, (dr, dc) in enumerate(DIRS):
            @pl.when(self.there(dr, dc))
            def _(d=d):
                self.copy(d).wait_send()


def reduce_stages(sizes, width, planes, col_early):
    groups = [[], []]
    for axis in range(2):
        mask, left = 1, sizes[axis]
        while left > 1:
            radix = 4 if left % 4 == 0 and not (axis == 0 and mask == 1) else 2
            groups[axis].append((axis, mask, radix))
            mask, left = mask * radix, left // radix
    first = 1 if col_early else len(groups[0])
    stages, rows = [], width
    for axis, mask, radix in groups[0][:first] + groups[1] + groups[0][first:]:
        kind = "full"
        if axis == 0 and rows % (8 * radix) == 0:
            kind, rows = "rows", rows // radix
        elif axis == 1 and planes % radix == 0:
            kind, planes = "planes", planes // radix
        stages.append((axis, mask, radix, kind, rows, planes))
    return stages


def held_shape(stages, s, width, light):
    _, _, _, _, rows, planes = stages[s]
    if s + 1 < len(stages) and stages[s + 1][3] == "planes":
        radix = stages[s + 1][2]
        return (radix, planes // radix + light, rows, width)
    return (planes + light, rows, width)


class ProbeSum:
    def __init__(self, me, stages, sums_ref, light, scale_ref, modes_ref, new_ref, landing, held, sems):
        self.me, self.stages, self.light, self.scale_ref = me, stages, light, scale_ref
        self.modes_ref, self.new_ref = modes_ref, new_ref
        self.landing, self.held = landing, [sums_ref] + list(held)
        self.send_sem, self.recv_sem, self.spread_send, self.spread_recv = sems
        self.digits, self.where, self.pending = [], [(jnp.int32(0), jnp.int32(0))], []
        for axis, mask, radix, kind, rows, planes in stages:
            digit = (me[axis] // mask) % radix
            row_off, plane_off = self.where[-1]
            if kind == "rows":
                row_off = row_off + digit * rows
            elif kind == "planes":
                plane_off = plane_off + digit * planes
            self.digits.append(digit)
            self.where.append((row_off, plane_off))

    def partner(self, s, j):
        axis, mask, radix = self.stages[s][:3]
        other = (self.digits[s] + j) % radix
        place = self.me[axis] + mask * (other - self.digits[s])
        return other, ((place, self.me[1]) if axis == 0 else (self.me[0], place))

    def piece(self, s, digit):
        kind, rows = self.stages[s][3:5]
        source = self.held[s]
        if kind == "rows":
            return source.at[:, pl.ds(pl.multiple_of(digit * rows, 8), rows), :]
        return source.at[digit] if kind == "planes" else source

    def copy(self, s, j):
        kind = self.stages[s][3]
        other, device = self.partner(s, j)
        slot = self.digits[s] if kind == "full" else j - 1
        return pltpu.make_async_remote_copy(
            src_ref=self.piece(s, other), dst_ref=self.landing[s].at[slot],
            send_sem=self.send_sem.at[s, j - 1], recv_sem=self.recv_sem.at[s, j - 1],
            device_id=device, device_id_type=MESH,
        )

    def start(self, s):
        for j in range(1, self.stages[s][2]):
            copy = self.copy(s, j)
            copy.start()
            self.pending.append(copy)

    def finish(self, s):
        _, _, radix, kind, _, planes = self.stages[s]
        own = self.piece(s, self.digits[s])[...]
        landing = self.landing[s]
        if kind == "full":
            landing[self.digits[s]] = own
        for j in range(1, radix):
            self.copy(s, j).wait_recv()
        if kind == "full":
            value = sum(landing[i] for i in range(radix))
        else:
            value = own + sum(landing[i] for i in range(radix - 1))
        target = self.held[s + 1]
        if s + 1 < len(self.stages) and self.stages[s + 1][3] == "planes":
            groups = self.stages[s + 1][2]
            each = planes // groups
            for g in range(groups):
                target[g, :each] = value[g * each : (g + 1) * each]
                if self.light:
                    target[g, each] = value[planes]
        else:
            target[...] = value

    def region(self, s):
        row_off, plane_off = self.where[s + 1]
        rows, planes = self.stages[s][4:]
        return pl.ds(plane_off, planes), pl.ds(pl.multiple_of(row_off, 8), rows), slice(None)

    def update(self):
        final = len(self.stages) - 1
        value = self.held[-1]
        planes = self.stages[final][5]
        place = self.region(final)
        if self.light:
            self.scale_ref[...] = 0.25 / jnp.sqrt(value[planes])
        self.new_ref[place] = self.modes_ref[place] - value[:planes] * self.scale_ref[...][None]

    def spread_stages(self):
        return [s for s in reversed(range(len(self.stages))) if self.stages[s][3] != "full"]

    def spread_copies(self, s):
        part = self.new_ref.at[self.region(s)]
        return [
            pltpu.make_async_remote_copy(
                src_ref=part, dst_ref=part, send_sem=self.spread_send.at[s, j - 1],
                recv_sem=self.spread_recv.at[s, j - 1], device_id=self.partner(s, j)[1], device_id_type=MESH,
            )
            for j in range(1, self.stages[s][2])
        ]

    def spread_start(self, s):
        copies = self.spread_copies(s)
        for copy in copies:
            copy.start()
        self.pending += copies

    def spread_finish(self, s):
        for copy in self.spread_copies(s):
            copy.wait_recv()

    def drain(self):
        for copy in self.pending:
            copy.wait_send()


def exchange_kernel(sizes, has_sums, has_halo, stages, row_off, *refs):
    refs = list(refs)
    take = lambda n: [refs.pop(0) for _ in range(n)]
    (obj_ref,) = take(1)
    if has_sums:
        grad_ref, gl_ref, gr_ref, sums_ref, modes_ref = take(5)
    if has_halo:
        center_ref, left_ref, right_ref = take(3)
    else:
        (out_ref,) = take(1)
    if has_sums:
        (new_modes_ref,) = take(1)
    if has_halo:
        pack_l, pack_r, halo_send, halo_recv = take(4)
    if has_sums:
        total, from_u, from_d, from_l, from_r, from_ul, from_ur, from_dl, from_dr = take(9)
        rim_send, rim_recv = take(2)
        (scale_ref,) = take(1)
        scratch = [(take(4), take(len(part)), take(len(part))) for part in stages]

    r, c = lax.axis_index("row"), lax.axis_index("col")
    me = (r, c)
    if has_halo:
        tile_rows, tile_cols = center_ref.shape[1] // 2, center_ref.shape[2]
        width = left_ref.shape[-1]
    else:
        tile_rows, tile_cols = out_ref.shape[1], out_ref.shape[2]
        width = gl_ref.shape[-1]
    half = width // 2
    lane = lax.broadcasted_iota(jnp.int32, (tile_rows, width), 1)

    near = Neighbours(sizes, me, None, None, None)
    barrier = pltpu.get_barrier_semaphore()
    expected = 0
    for dr, dc in DIRS:
        cond = near.there(dr, dc)
        expected = expected + cond.astype(jnp.int32)

        @pl.when(cond)
        def _(dr=dr, dc=dc):
            pl.semaphore_signal(barrier, inc=1, device_id=(r + dr, c + dc), device_id_type=MESH)

    if has_sums:
        planes = modes_ref.shape[0]
        cut = planes // 2
        parts = []
        for part, first, last in ((0, cut, planes), (1, 0, cut)):
            sems, landing, held = scratch[part]
            light = 1 - part
            parts.append(ProbeSum(
                me, stages[part], sums_ref.at[first : last + light], light, scale_ref,
                modes_ref.at[first:last], new_modes_ref.at[first:last], landing, held, sems,
            ))
        for s in range(len(stages[0])):
            for j in range(1, stages[0][s][2]):
                _, device = parts[0].partner(s, j)
                pl.semaphore_signal(barrier, inc=1, device_id=device, device_id_type=MESH)
                expected = expected + 1
    pl.semaphore_wait(barrier, expected)

    if has_sums:
        top, bottom = slice(0, half), slice(tile_rows + half, tile_rows + width)
        inner = slice(half, tile_rows + half)
        cols = slice(width, width + tile_cols)
        rims = Neighbours(sizes, me, [
            (grad_ref.at[:, top, cols], from_d),
            (grad_ref.at[:, bottom, cols], from_u),
            (gl_ref.at[:, inner, :], from_r),
            (gr_ref.at[:, inner, :], from_l),
            (gl_ref.at[:, top, :], from_dr),
            (gr_ref.at[:, top, :], from_dl),
            (gl_ref.at[:, bottom, :], from_ur),
            (gr_ref.at[:, bottom, :], from_ul),
        ], rim_send, rim_recv)
        count = len(stages[0])
        for part in parts:
            part.start(0)
        for part in parts:
            part.finish(0)
            if count > 1:
                part.start(1)
        rims.start()
        total[...] = grad_ref[:, inner, cols]

        def add_rim(d):
            if d == 0:
                total[:, tile_rows - half :, :] += from_d[...]
            elif d == 1:
                total[:, :half, :] += from_u[...]
            else:
                source, rows = {
                    2: (from_r, slice(0, tile_rows)), 3: (from_l, slice(0, tile_rows)),
                    4: (from_dr, slice(tile_rows - half, tile_rows)),
                    5: (from_dl, slice(tile_rows - half, tile_rows)),
                    6: (from_ur, slice(0, half)), 7: (from_ul, slice(0, half)),
                }[d]
                side = lane[rows]
                for q in range(2):
                    value = source[q]
                    turned = pltpu.roll(value, half, 1)
                    if d in (3, 5, 7):
                        total[q, rows, :width] += jnp.where(side < half, value, 0.0)
                        total[q + 2, rows, :width] += jnp.where(side < half, turned, 0.0)
                    else:
                        total[q, rows, tile_cols - width :] += jnp.where(side >= half, turned, 0.0)
                        total[q + 2, rows, tile_cols - width :] += jnp.where(side >= half, value, 0.0)

        def reduce_step(s):
            for part in parts:
                part.finish(s)
                if s + 1 < count:
                    part.start(s + 1)

        def spread_step(n):
            for part, order in zip(parts, orders):
                if n == 0:
                    part.update()
                else:
                    part.spread_finish(order[n - 1])
                if n < len(order):
                    part.spread_start(order[n])

        orders = [part.spread_stages() for part in parts]
        early = 2 if has_halo else count
        for s in range(1, early):
            reduce_step(s)
        if not has_halo:
            spread_step(0)
        rims.wait_recv(add_rim)
        new = obj_ref[:, row_off : row_off + tile_rows, :] - 0.1 * total[...]
    else:
        new = obj_ref[...]

    if has_halo:
        center_ref[:, half : half + tile_rows, :] = new
        for q in range(2):
            lower, upper = new[q], new[q + 2]
            pack_l[q] = jnp.where(lane < half, lower[:, :width], pltpu.roll(upper[:, :width], half, 1))
            pack_r[q] = jnp.where(
                lane < half, pltpu.roll(lower[:, tile_cols - width :], half, 1), upper[:, tile_cols - width :]
            )
        first, final = slice(0, half), slice(tile_rows + half, tile_rows + width)
        middle = slice(half, half + tile_rows)
        ends = slice(tile_rows - half, tile_rows)
        halos = Neighbours(sizes, me, [
            (center_ref.at[:, half:width, :], center_ref.at[:, final, :]),
            (center_ref.at[:, tile_rows : tile_rows + half, :], center_ref.at[:, first, :]),
            (pack_l, right_ref.at[:, middle, :]),
            (pack_r, left_ref.at[:, middle, :]),
            (pack_l.at[:, first, :], right_ref.at[:, final, :]),
            (pack_r.at[:, first, :], left_ref.at[:, final, :]),
            (pack_l.at[:, ends, :], right_ref.at[:, first, :]),
            (pack_r.at[:, ends, :], left_ref.at[:, first, :]),
        ], halo_send, halo_recv)
        halos.start()
    else:
        out_ref[...] = new

    if has_sums:
        for s in range(early, count):
            reduce_step(s)
        for n in range(0 if has_halo else 1, len(orders[0]) + 1):
            spread_step(n)
        for part in parts:
            part.drain()
        rims.wait_send()
    if has_halo:
        halos.wait_recv()
        halos.wait_send()


def exchange(sizes, tile, width, ident, obj, sums=None, halo=True, row_off=0):
    tile_rows, tile_cols = tile
    half = width // 2
    rows = tile_rows + width
    vmem = pl.BlockSpec(memory_space=pltpu.VMEM)
    shape = lambda *s: jax.ShapeDtypeStruct(s, jnp.float32)
    buf = lambda *s: pltpu.VMEM(s, jnp.float32)
    dma = lambda *n: pltpu.SemaphoreType.DMA(n)
    operands, outs, scratch, stages = [obj], [], [], []
    specs = [vmem]
    if halo:
        outs += [shape(4, rows, tile_cols), shape(2, rows, width), shape(2, rows, width)]
    else:
        outs += [shape(4, tile_rows, tile_cols)]
    if halo:
        scratch += [buf(2, tile_rows, width), buf(2, tile_rows, width), dma(8), dma(8)]
    if sums is not None:
        operands += list(sums)
        specs += [vmem] * len(sums)
        planes = sums[-1].shape[0]
        outs += [shape(planes, width, width)]
        stages = [reduce_stages(sizes, width, planes // 2, col_early) for col_early in (False, True)]
        scratch += [
            buf(4, tile_rows, tile_cols),
            buf(4, half, tile_cols), buf(4, half, tile_cols),
            buf(2, tile_rows, width), buf(2, tile_rows, width),
            buf(2, half, width), buf(2, half, width), buf(2, half, width), buf(2, half, width),
            dma(8), dma(8), buf(stages[0][-1][4], width),
        ]
        for part, light in zip(stages, (1, 0)):
            scratch += [dma(len(part), 3) for _ in range(4)]
            for _, _, radix, kind, rows_held, planes_held in part:
                slots = radix if kind == "full" else radix - 1
                scratch.append(buf(slots, planes_held + light, rows_held, width))
            scratch += [buf(*held_shape(part, s, width, light)) for s in range(len(part))]
    return pl.pallas_call(
        functools.partial(exchange_kernel, sizes, sums is not None, halo, stages, row_off),
        out_shape=tuple(outs),
        in_specs=specs,
        out_specs=(vmem,) * len(outs),
        scratch_shapes=scratch,
        compiler_params=pltpu.CompilerParams(
            collective_id=ident, has_side_effects=True, vmem_limit_bytes=EXCHANGE_BYTES
        ),
        cost_estimate=pl.CostEstimate(flops=0, transcendentals=0, bytes_accessed=32 * 1024 * 1024),
        name="exchange_%d" % ident,
    )(*operands)


def body(sizes, objects, probe_modes, intensities, positions, counts):
    width = probe_modes.shape[-1]
    tile = objects.shape[2:]
    tables = jnp.asarray(transform_tables(width))
    modes = probe_modes.reshape(-1, width, width)
    measured = intensities[0, 0]
    extended = exchange(sizes, tile, width, 0, objects.reshape((4,) + tile))
    for step in range(ITERS):
        final = step == ITERS - 1
        sums = local_pass(
            extended, modes, measured, positions[0, 0], counts, tables, tile, exact=not final
        )
        result = exchange(
            sizes, tile, width, step + 1, extended[0], tuple(sums) + (modes,),
            halo=not final, row_off=width // 2,
        )
        modes = result[-1]
        extended = result[:-1]
    return extended[0].reshape(objects.shape), modes.reshape(probe_modes.shape)


def solution(mesh):
    sizes = (mesh.shape["row"], mesh.shape["col"])
    return jax.shard_map(
        functools.partial(body, sizes),
        mesh=mesh,
        in_specs=(
            P(None, None, "row", "col"),
            P(),
            P("row", "col", None, None, None),
            P("row", "col", None, None),
            P("row", "col"),
        ),
        out_specs=(P(None, None, "row", "col"), P()),
        check_vma=False,
    )
```

```python
import functools
import math

import jax
import jax.numpy as jnp
import ml_dtypes
import numpy as np
from jax import lax
from jax.experimental import pallas as pl
from jax.experimental.pallas import tpu as pltpu
from jax.sharding import PartitionSpec as P

ITERS = 2
EIGHT = 8.0
PASS_BYTES = 32 * 1024 * 1024
EXCHANGE_BYTES = 24 * 1024 * 1024
MESH = pl.DeviceIdType.MESH
DIRS = ((-1, 0), (1, 0), (0, -1), (0, 1), (-1, -1), (-1, 1), (1, -1), (1, 1))


def real_block(table):
    return np.block([[table.real, -table.imag], [table.imag, table.real]])


def transform_tables(width):
    index = np.arange(width)
    product = np.outer(index, index) % width
    turns = np.exp(-2j * math.pi * product / width)
    far = turns / math.sqrt(width)
    frequency = (index + width // 2) % width - width // 2
    factor = np.exp(-4j * math.pi * frequency.astype(np.float64) ** 2 / width**2)
    step = far.conj() @ (factor[:, None] * far)
    step = (step + step.T) / 2
    blocks = np.stack([real_block(turns / EIGHT), real_block(turns / EIGHT).T, real_block(step), real_block(step).T])
    parts = []
    for _ in range(3):
        parts.append(blocks.astype(ml_dtypes.bfloat16))
        blocks = blocks - parts[-1].astype(np.float64)
    return np.concatenate([np.concatenate(parts[:2]), parts[2][2:3]])


def split_parts(value):
    high = value.astype(jnp.bfloat16)
    return high, (value - high.astype(jnp.float32)).astype(jnp.bfloat16)


def dot(first, second):
    return jnp.dot(first, second, preferred_element_type=jnp.float32)


def products(tab_ref, place, value, table_first, exact):
    high, low = split_parts(value)
    pairs = [(0, high), (0, low), (1, high)] + ([(2, high)] if exact else [])
    total = None
    for part, operand in pairs:
        table = tab_ref[4 * part + (place if part < 2 else 0)]
        term = dot(table, operand) if table_first else dot(operand, table)
        total = term if total is None else total + term
    return total


def apply_transform(tab_ref, left, fields, exact):
    right = left + 1 if left % 2 == 0 else left - 1
    width = fields[0][0].shape[0]
    stacked = jnp.concatenate([jnp.concatenate([r, i], axis=0) for r, i in fields], axis=1)
    upper = products(tab_ref, left, stacked, True, exact)
    rows = []
    for m in range(len(fields)):
        cols = slice(m * width, (m + 1) * width)
        rows.append(jnp.concatenate([upper[:width, cols], upper[width:, cols]], axis=1))
    out = products(tab_ref, right, jnp.concatenate(rows, axis=0), False, exact)
    return [
        (out[m * width : (m + 1) * width, :width], out[m * width : (m + 1) * width, width:])
        for m in range(len(fields))
    ]


def times(a, b):
    return (a[0] * b[0] - a[1] * b[1], a[0] * b[1] + a[1] * b[0])


def conj_times(a, b):
    return (a[0] * b[0] + a[1] * b[1], a[0] * b[1] - a[1] * b[0])


def pass_kernel(
    tile, exact, pos_ref, cnt_ref, center_ref, left_ref, right_ref, modes_ref, meas_ref, tab_ref,
    grad_ref, gl_ref, gr_ref, sums_ref, ext,
):
    tile_rows, tile_cols = tile
    width = meas_ref.shape[-1]
    half = width // 2
    modes = sums_ref.shape[0] // 2
    slots = meas_ref.shape[0] - 2 * modes
    last = width + tile_cols
    ext[:, :, width:last] = center_ref[...]
    for q in range(2):
        ext[q, :, :width] = pltpu.roll(left_ref[q], half, 1)
        ext[q + 2, :, :width] = left_ref[q]
        ext[q, :, last:] = right_ref[q]
        ext[q + 2, :, last:] = pltpu.roll(right_ref[q], half, 1)
    grad_ref[...] = jnp.zeros_like(grad_ref)
    sums_ref[...] = jnp.zeros_like(sums_ref)
    row0 = lax.axis_index("row") * tile_rows - half
    col0 = lax.axis_index("col") * tile_cols - width
    lane = lax.broadcasted_iota(jnp.int32, (width, width), 1)
    tall_lane = lax.broadcasted_iota(jnp.int32, (width + 8, width), 1)

    factor = EIGHT * EIGHT / width
    probe = lambda: [(modes_ref[2 * m], modes_ref[2 * m + 1]) for m in range(modes)]

    class Slot:
        def __init__(self, k):
            self.k = k
            row = pos_ref[k, 0] - row0
            col = pos_ref[k, 1] - col0
            self.base = pl.multiple_of((col // width) * width, width)
            self.shift = col % width
            self.top = pl.multiple_of((row // 8) * 8, 8)
            self.down = row % 8
            self.o0 = (self.cut(0), self.cut(1))
            self.o1 = (self.cut(2), self.cut(3))

        def cut(self, p):
            window = ext[p, pl.ds(self.top, width + 8), pl.ds(self.base, 2 * width)]
            window = pltpu.roll(window, (width + 8 - self.down) % (width + 8), 0)[:width]
            back = (width - self.shift) % width
            first = pltpu.roll(window[:, :width], back, 1)
            second = pltpu.roll(window[:, width:], back, 1)
            return jnp.where(lane < width - self.shift, first, second)

        def add_patch(self, p, value):
            value = jnp.concatenate([value, jnp.zeros((8, width), jnp.float32)], axis=0)
            rolled = pltpu.roll(pltpu.roll(value, self.down, 0), self.shift, 1)
            rows = pl.ds(self.top, width + 8)
            grad_ref[p, rows, pl.ds(self.base, width)] += jnp.where(tall_lane >= self.shift, rolled, 0.0)
            after = pl.multiple_of(self.base + width, width)
            grad_ref[p, rows, pl.ds(after, width)] += jnp.where(tall_lane < self.shift, rolled, 0.0)

        def forward(self):
            self.waves = apply_transform(tab_ref, 2, [times(p, self.o0) for p in probe()], exact)

        def far_field(self):
            self.far = apply_transform(tab_ref, 0, [times(w, self.o1) for w in self.waves], False)

        def far_back(self):
            intensity = sum(r * r + i * i for r, i in self.far) * (factor * factor)
            weight = (2.0 * factor * factor) * (intensity - meas_ref[2 * modes + self.k])
            fields = [(weight * r, weight * i) for r, i in self.far]
            self.grads = apply_transform(tab_ref, 1, fields, False)

        def back(self):
            terms = [conj_times(w, g) for w, g in zip(self.waves, self.grads)]
            self.add_patch(2, sum(t[0] for t in terms))
            self.add_patch(3, sum(t[1] for t in terms))
            fields = [conj_times(self.o1, g) for g in self.grads]
            self.grads = apply_transform(tab_ref, 3, fields, False)

        def finish(self):
            terms = [conj_times(p, g) for p, g in zip(probe(), self.grads)]
            self.add_patch(0, sum(t[0] for t in terms))
            self.add_patch(1, sum(t[1] for t in terms))
            for m in range(modes):
                term = conj_times(self.o0, self.grads[m])
                sums_ref[2 * m] += term[0]
                sums_ref[2 * m + 1] += term[1]
            sums_ref[2 * modes] += self.o0[0] * self.o0[0] + self.o0[1] * self.o0[1]

    def run(indices):
        group = [Slot(k) for k in indices]
        for phase in (Slot.forward, Slot.far_field, Slot.far_back, Slot.back, Slot.finish):
            for one in group:
                phase(one)

    count = cnt_ref[0, 0]

    @pl.when(count == slots)
    def _():
        run(range(slots))

    @pl.when(count < slots)
    def _():
        def alone(k, carry):
            @pl.when(k < count)
            def _():
                run([k])

            return carry

        lax.fori_loop(0, slots - 1, alone, 0)

    lane = lax.broadcasted_iota(jnp.int32, (grad_ref.shape[1], width), 1)
    for q in range(2):
        gl_ref[q] = jnp.where(
            lane < half, pltpu.roll(grad_ref[q, :, :width], half, 1), grad_ref[q + 2, :, :width]
        )
        gr_ref[q] = jnp.where(
            lane < half, grad_ref[q, :, last:], pltpu.roll(grad_ref[q + 2, :, last:], half, 1)
        )


def local_pass(extended, modes, planes, given, positions, counts, tables, tile, exact):
    center, left, right = extended
    rows = center.shape[1]
    width = given.shape[-1]
    wide = center.shape[2] + 2 * width
    smem = pl.BlockSpec(memory_space=pltpu.SMEM)
    vmem = pl.BlockSpec(memory_space=pltpu.VMEM)
    shape = lambda *s: jax.ShapeDtypeStruct(s, jnp.float32)
    return pl.pallas_call(
        functools.partial(pass_kernel, tile, exact),
        out_shape=(
            shape(4, rows, wide),
            shape(2, rows, width),
            shape(2, rows, width),
            shape(planes + 1, width, width),
        ),
        in_specs=[smem, smem] + [vmem] * 6,
        out_specs=(vmem,) * 4,
        scratch_shapes=[pltpu.VMEM((4, rows, wide), jnp.float32)],
        compiler_params=pltpu.CompilerParams(vmem_limit_bytes=PASS_BYTES),
        name="local_pass",
    )(positions, counts, center, left, right, modes, given, tables)


class Neighbours:
    def __init__(self, sizes, me, pieces, send_sems, recv_sems):
        self.sizes, self.me, self.pieces = sizes, me, pieces
        self.send_sems, self.recv_sems = send_sems, recv_sems

    def there(self, dr, dc):
        (rows, cols), (r, c) = self.sizes, self.me
        found = None
        for cond in (
            [r > 0] if dr < 0 else [r < rows - 1] if dr > 0 else []
        ) + ([c > 0] if dc < 0 else [c < cols - 1] if dc > 0 else []):
            found = cond if found is None else jnp.logical_and(found, cond)
        return found

    def copy(self, d):
        dr, dc = DIRS[d]
        src, dst = self.pieces[d]
        return pltpu.make_async_remote_copy(
            src_ref=src, dst_ref=dst, send_sem=self.send_sems.at[d], recv_sem=self.recv_sems.at[d],
            device_id=(self.me[0] + dr, self.me[1] + dc), device_id_type=MESH,
        )

    def start(self):
        for d, (dr, dc) in enumerate(DIRS):
            @pl.when(self.there(dr, dc))
            def _(d=d):
                self.copy(d).start()

    def wait_recv(self, after=None):
        for d, (dr, dc) in enumerate(DIRS):
            @pl.when(self.there(-dr, -dc))
            def _(d=d):
                self.copy(d).wait_recv()
                if after is not None:
                    after(d)

    def wait_send(self):
        for d, (dr, dc) in enumerate(DIRS):
            @pl.when(self.there(dr, dc))
            def _(d=d):
                self.copy(d).wait_send()


def reduce_stages(sizes, width, planes, col_early):
    groups = [[], []]
    for axis in range(2):
        mask, left = 1, sizes[axis]
        while left > 1:
            radix = 4 if left % 4 == 0 and not (axis == 0 and mask == 1) else 2
            groups[axis].append((axis, mask, radix))
            mask, left = mask * radix, left // radix
    first = 1 if col_early else len(groups[0])
    stages, rows = [], width
    for axis, mask, radix in groups[0][:first] + groups[1] + groups[0][first:]:
        kind = "full"
        if axis == 0 and rows % (8 * radix) == 0:
            kind, rows = "rows", rows // radix
        elif axis == 1 and planes % radix == 0:
            kind, planes = "planes", planes // radix
        stages.append((axis, mask, radix, kind, rows, planes))
    return stages


def held_shape(stages, s, width, light):
    _, _, _, _, rows, planes = stages[s]
    if s + 1 < len(stages) and stages[s + 1][3] == "planes":
        radix = stages[s + 1][2]
        return (radix, planes // radix + light, rows, width)
    return (planes + light, rows, width)


class ProbeSum:
    def __init__(self, me, stages, sums_ref, light, scale_ref, modes_ref, new_ref, landing, held, sems):
        self.me, self.stages, self.light, self.scale_ref = me, stages, light, scale_ref
        self.modes_ref, self.new_ref = modes_ref, new_ref
        self.landing, self.held = landing, [sums_ref] + list(held)
        self.send_sem, self.recv_sem, self.spread_send, self.spread_recv = sems
        self.digits, self.where, self.pending = [], [(jnp.int32(0), jnp.int32(0))], []
        for axis, mask, radix, kind, rows, planes in stages:
            digit = (me[axis] // mask) % radix
            row_off, plane_off = self.where[-1]
            if kind == "rows":
                row_off = row_off + digit * rows
            elif kind == "planes":
                plane_off = plane_off + digit * planes
            self.digits.append(digit)
            self.where.append((row_off, plane_off))

    def partner(self, s, j):
        axis, mask, radix = self.stages[s][:3]
        other = (self.digits[s] + j) % radix
        place = self.me[axis] + mask * (other - self.digits[s])
        return other, ((place, self.me[1]) if axis == 0 else (self.me[0], place))

    def piece(self, s, digit):
        kind, rows = self.stages[s][3:5]
        source = self.held[s]
        if kind == "rows":
            return source.at[:, pl.ds(pl.multiple_of(digit * rows, 8), rows), :]
        return source.at[digit] if kind == "planes" else source

    def copy(self, s, j):
        kind = self.stages[s][3]
        other, device = self.partner(s, j)
        slot = self.digits[s] if kind == "full" else j - 1
        return pltpu.make_async_remote_copy(
            src_ref=self.piece(s, other), dst_ref=self.landing[s].at[slot],
            send_sem=self.send_sem.at[s, j - 1], recv_sem=self.recv_sem.at[s, j - 1],
            device_id=device, device_id_type=MESH,
        )

    def start(self, s):
        for j in range(1, self.stages[s][2]):
            copy = self.copy(s, j)
            copy.start()
            self.pending.append(copy)

    def finish(self, s):
        _, _, radix, kind, _, planes = self.stages[s]
        own = self.piece(s, self.digits[s])[...]
        landing = self.landing[s]
        if kind == "full":
            landing[self.digits[s]] = own
        for j in range(1, radix):
            self.copy(s, j).wait_recv()
        if kind == "full":
            value = sum(landing[i] for i in range(radix))
        else:
            value = own + sum(landing[i] for i in range(radix - 1))
        target = self.held[s + 1]
        if s + 1 < len(self.stages) and self.stages[s + 1][3] == "planes":
            groups = self.stages[s + 1][2]
            each = planes // groups
            for g in range(groups):
                target[g, :each] = value[g * each : (g + 1) * each]
                if self.light:
                    target[g, each] = value[planes]
        else:
            target[...] = value

    def region(self, s):
        row_off, plane_off = self.where[s + 1]
        rows, planes = self.stages[s][4:]
        return pl.ds(plane_off, planes), pl.ds(pl.multiple_of(row_off, 8), rows), slice(None)

    def update(self):
        final = len(self.stages) - 1
        value = self.held[-1]
        planes = self.stages[final][5]
        place = self.region(final)
        if self.light:
            self.scale_ref[...] = 0.25 / jnp.sqrt(value[planes])
        self.new_ref[place] = self.modes_ref[place] - value[:planes] * self.scale_ref[...][None]

    def spread_stages(self):
        return [s for s in reversed(range(len(self.stages))) if self.stages[s][3] != "full"]

    def spread_copies(self, s):
        part = self.new_ref.at[self.region(s)]
        return [
            pltpu.make_async_remote_copy(
                src_ref=part, dst_ref=part, send_sem=self.spread_send.at[s, j - 1],
                recv_sem=self.spread_recv.at[s, j - 1], device_id=self.partner(s, j)[1], device_id_type=MESH,
            )
            for j in range(1, self.stages[s][2])
        ]

    def spread_start(self, s):
        copies = self.spread_copies(s)
        for copy in copies:
            copy.start()
        self.pending += copies

    def spread_finish(self, s):
        for copy in self.spread_copies(s):
            copy.wait_recv()

    def drain(self):
        for copy in self.pending:
            copy.wait_send()


def exchange_kernel(sizes, has_sums, has_halo, stages, row_off, *refs):
    refs = list(refs)
    take = lambda n: [refs.pop(0) for _ in range(n)]
    (obj_ref,) = take(1)
    if has_sums:
        grad_ref, gl_ref, gr_ref, sums_ref, modes_ref = take(5)
    if has_halo:
        center_ref, left_ref, right_ref = take(3)
    else:
        (out_ref,) = take(1)
    if has_sums:
        (new_modes_ref,) = take(1)
    if has_halo:
        pack_l, pack_r, halo_send, halo_recv = take(4)
    if has_sums:
        total, from_u, from_d, from_l, from_r, from_ul, from_ur, from_dl, from_dr = take(9)
        rim_send, rim_recv = take(2)
        (scale_ref,) = take(1)
        scratch = [(take(4), take(len(part)), take(len(part))) for part in stages]

    r, c = lax.axis_index("row"), lax.axis_index("col")
    me = (r, c)
    if has_halo:
        tile_rows, tile_cols = center_ref.shape[1] // 2, center_ref.shape[2]
        width = left_ref.shape[-1]
    else:
        tile_rows, tile_cols = out_ref.shape[1], out_ref.shape[2]
        width = gl_ref.shape[-1]
    half = width // 2
    lane = lax.broadcasted_iota(jnp.int32, (tile_rows, width), 1)

    near = Neighbours(sizes, me, None, None, None)
    barrier = pltpu.get_barrier_semaphore()
    expected = 0
    for dr, dc in DIRS:
        cond = near.there(dr, dc)
        expected = expected + cond.astype(jnp.int32)

        @pl.when(cond)
        def _(dr=dr, dc=dc):
            pl.semaphore_signal(barrier, inc=1, device_id=(r + dr, c + dc), device_id_type=MESH)

    if has_sums:
        planes = modes_ref.shape[0]
        cut = planes // 2
        parts = []
        for part, first, last in ((0, cut, planes), (1, 0, cut)):
            sems, landing, held = scratch[part]
            light = 1 - part
            parts.append(ProbeSum(
                me, stages[part], sums_ref.at[first : last + light], light, scale_ref,
                modes_ref.at[first:last], new_modes_ref.at[first:last], landing, held, sems,
            ))
        for s in range(len(stages[0])):
            for j in range(1, stages[0][s][2]):
                _, device = parts[0].partner(s, j)
                pl.semaphore_signal(barrier, inc=1, device_id=device, device_id_type=MESH)
                expected = expected + 1
    pl.semaphore_wait(barrier, expected)

    if has_sums:
        top, bottom = slice(0, half), slice(tile_rows + half, tile_rows + width)
        inner = slice(half, tile_rows + half)
        cols = slice(width, width + tile_cols)
        rims = Neighbours(sizes, me, [
            (grad_ref.at[:, top, cols], from_d),
            (grad_ref.at[:, bottom, cols], from_u),
            (gl_ref.at[:, inner, :], from_r),
            (gr_ref.at[:, inner, :], from_l),
            (gl_ref.at[:, top, :], from_dr),
            (gr_ref.at[:, top, :], from_dl),
            (gl_ref.at[:, bottom, :], from_ur),
            (gr_ref.at[:, bottom, :], from_ul),
        ], rim_send, rim_recv)
        count = len(stages[0])
        for part in parts:
            part.start(0)
        for part in parts:
            part.finish(0)
            if count > 1:
                part.start(1)
        rims.start()
        total[...] = grad_ref[:, inner, cols]

        def add_rim(d):
            if d == 0:
                total[:, tile_rows - half :, :] += from_d[...]
            elif d == 1:
                total[:, :half, :] += from_u[...]
            else:
                source, rows = {
                    2: (from_r, slice(0, tile_rows)), 3: (from_l, slice(0, tile_rows)),
                    4: (from_dr, slice(tile_rows - half, tile_rows)),
                    5: (from_dl, slice(tile_rows - half, tile_rows)),
                    6: (from_ur, slice(0, half)), 7: (from_ul, slice(0, half)),
                }[d]
                side = lane[rows]
                for q in range(2):
                    value = source[q]
                    turned = pltpu.roll(value, half, 1)
                    if d in (3, 5, 7):
                        total[q, rows, :width] += jnp.where(side < half, value, 0.0)
                        total[q + 2, rows, :width] += jnp.where(side < half, turned, 0.0)
                    else:
                        total[q, rows, tile_cols - width :] += jnp.where(side >= half, turned, 0.0)
                        total[q + 2, rows, tile_cols - width :] += jnp.where(side >= half, value, 0.0)

        def reduce_step(s):
            for part in parts:
                part.finish(s)
                if s + 1 < count:
                    part.start(s + 1)

        def spread_step(n):
            for part, order in zip(parts, orders):
                if n == 0:
                    part.update()
                else:
                    part.spread_finish(order[n - 1])
                if n < len(order):
                    part.spread_start(order[n])

        orders = [part.spread_stages() for part in parts]
        early = 2 if has_halo else count
        for s in range(1, early):
            reduce_step(s)
        if not has_halo:
            spread_step(0)
        rims.wait_recv(add_rim)
        new = obj_ref[:, row_off : row_off + tile_rows, :] - 0.1 * total[...]
    else:
        new = obj_ref[...]

    if has_halo:
        center_ref[:, half : half + tile_rows, :] = new
        for q in range(2):
            lower, upper = new[q], new[q + 2]
            pack_l[q] = jnp.where(lane < half, lower[:, :width], pltpu.roll(upper[:, :width], half, 1))
            pack_r[q] = jnp.where(
                lane < half, pltpu.roll(lower[:, tile_cols - width :], half, 1), upper[:, tile_cols - width :]
            )
        first, final = slice(0, half), slice(tile_rows + half, tile_rows + width)
        middle = slice(half, half + tile_rows)
        ends = slice(tile_rows - half, tile_rows)
        halos = Neighbours(sizes, me, [
            (center_ref.at[:, half:width, :], center_ref.at[:, final, :]),
            (center_ref.at[:, tile_rows : tile_rows + half, :], center_ref.at[:, first, :]),
            (pack_l, right_ref.at[:, middle, :]),
            (pack_r, left_ref.at[:, middle, :]),
            (pack_l.at[:, first, :], right_ref.at[:, final, :]),
            (pack_r.at[:, first, :], left_ref.at[:, final, :]),
            (pack_l.at[:, ends, :], right_ref.at[:, first, :]),
            (pack_r.at[:, ends, :], left_ref.at[:, first, :]),
        ], halo_send, halo_recv)
        halos.start()
    else:
        out_ref[...] = new

    if has_sums:
        for s in range(early, count):
            reduce_step(s)
        for n in range(0 if has_halo else 1, len(orders[0]) + 1):
            spread_step(n)
        for part in parts:
            part.drain()
        rims.wait_send()
    if has_halo:
        halos.wait_recv()
        halos.wait_send()


def exchange(sizes, tile, width, ident, obj, sums=None, halo=True, row_off=0):
    tile_rows, tile_cols = tile
    half = width // 2
    rows = tile_rows + width
    vmem = pl.BlockSpec(memory_space=pltpu.VMEM)
    shape = lambda *s: jax.ShapeDtypeStruct(s, jnp.float32)
    buf = lambda *s: pltpu.VMEM(s, jnp.float32)
    dma = lambda *n: pltpu.SemaphoreType.DMA(n)
    operands, outs, scratch, stages = [obj], [], [], []
    specs = [vmem]
    if halo:
        outs += [shape(4, rows, tile_cols), shape(2, rows, width), shape(2, rows, width)]
    else:
        outs += [shape(4, tile_rows, tile_cols)]
    if halo:
        scratch += [buf(2, tile_rows, width), buf(2, tile_rows, width), dma(8), dma(8)]
    if sums is not None:
        operands += list(sums)
        specs += [vmem] * len(sums)
        planes = sums[-1].shape[0]
        outs += [shape(planes, width, width)]
        stages = [reduce_stages(sizes, width, planes // 2, col_early) for col_early in (False, True)]
        scratch += [
            buf(4, tile_rows, tile_cols),
            buf(4, half, tile_cols), buf(4, half, tile_cols),
            buf(2, tile_rows, width), buf(2, tile_rows, width),
            buf(2, half, width), buf(2, half, width), buf(2, half, width), buf(2, half, width),
            dma(8), dma(8), buf(stages[0][-1][4], width),
        ]
        for part, light in zip(stages, (1, 0)):
            scratch += [dma(len(part), 3) for _ in range(4)]
            for _, _, radix, kind, rows_held, planes_held in part:
                slots = radix if kind == "full" else radix - 1
                scratch.append(buf(slots, planes_held + light, rows_held, width))
            scratch += [buf(*held_shape(part, s, width, light)) for s in range(len(part))]
    return pl.pallas_call(
        functools.partial(exchange_kernel, sizes, sums is not None, halo, stages, row_off),
        out_shape=tuple(outs),
        in_specs=specs,
        out_specs=(vmem,) * len(outs),
        scratch_shapes=scratch,
        compiler_params=pltpu.CompilerParams(
            collective_id=ident, has_side_effects=True, vmem_limit_bytes=EXCHANGE_BYTES
        ),
        cost_estimate=pl.CostEstimate(flops=0, transcendentals=0, bytes_accessed=32 * 1024 * 1024),
        name="exchange_%d" % ident,
    )(*operands)


def body(sizes, objects, probe_modes, intensities, positions, counts):
    width = probe_modes.shape[-1]
    tile = objects.shape[2:]
    tables = jnp.asarray(transform_tables(width))
    modes = probe_modes.reshape(-1, width, width)
    planes = modes.shape[0]
    given = jnp.concatenate([modes, intensities[0, 0]])
    extended = exchange(sizes, tile, width, 0, objects.reshape((4,) + tile))
    for step in range(ITERS):
        final = step == ITERS - 1
        sums = local_pass(
            extended, modes if step else given, planes, given, positions[0, 0], counts, tables, tile,
            exact=not final,
        )
        result = exchange(
            sizes, tile, width, step + 1, extended[0], tuple(sums) + (modes,),
            halo=not final, row_off=width // 2,
        )
        modes = result[-1]
        extended = result[:-1]
    return extended[0].reshape(objects.shape), modes.reshape(probe_modes.shape)


def solution(mesh):
    sizes = (mesh.shape["row"], mesh.shape["col"])
    return jax.shard_map(
        functools.partial(body, sizes),
        mesh=mesh,
        in_specs=(
            P(None, None, "row", "col"),
            P(),
            P("row", "col", None, None, None),
            P("row", "col", None, None),
            P("row", "col"),
        ),
        out_specs=(P(None, None, "row", "col"), P()),
        check_vma=False,
    )
```
